1024 devices in a mesh: seq: 64 (over y, x, core), head: 16 (over z).
Axes of the slice: x: 4, y: 8, z: 16, core: 2. Of those that a mesh axis runs over, the one named last changes fastest.
Arguments:
- queries: bfloat16 [16384, 8192], P('seq', 'head'), may hold values from -8 to 8
- keys: bfloat16 [16384, 2048], P('seq', 'head'), may hold values from -8 to 8
- values: bfloat16 [16384, 2048], P('seq', 'head'), may hold values from -6 to 6
- grad_out: bfloat16 [16384, 8192], P('seq', 'head'), may hold values from -6 to 6
- gate: float32 [16384, 64], P('seq', 'head'), may hold values from 0.05 to 0.95
- gate_weight: bfloat16 [64, 7168], P(None, 'head'), may hold values from -0.75 to 0.75
- selection: int32 [256, 16, 16], P(None, 'head'), may hold values from -1 to 255, as said below
Outputs:
- grad_queries: bfloat16 [16384, 8192], P('seq', 'head')
- grad_keys: bfloat16 [16384, 2048], P('seq', 'head')
- grad_values: bfloat16 [16384, 2048], P('seq', 'head')
- grad_input: bfloat16 [16384, 7168], P('seq', 'head')
The draws below stay inside these ranges and needn't reach their ends.
Inputs may be any that keep to these rules, and one draw needn't show every extreme that they name: `selection`: row [c, g] lists distinct key blocks for query block c of group g, none after block c, always block c itself; -1 marks an unused entry, and such entries come last in a row. For one group and the 4 query blocks of one index of seq, all blocks named that lie on another index of seq are, for each such index, one and the same block.
All inputs are finite; a program needn't handle non-finite values.
Results may differ from the reference program's by a relative error of at most 0.038.
Values may be sent and summed in bfloat16 or wider, within the bound.
A program may use at most 64 MiB of HBM per device.

```python
import math
import jax
import jax.numpy as jnp
from jax import lax

D = 7168
HEAD_DIM = 128
GQA = 4
BLK = 64
SEL = 16
TOKENS = 16384
KVH = 16
HEADS = 64
QB_DEV = 4
NQB = 256
N_SEQ = 64


def draw_queries(key, part):
    base = jax.random.normal(jax.random.fold_in(key, 1), (TOKENS, HEADS * HEAD_DIM), jnp.float32)
    return jnp.clip(base, -8.0, 8.0).astype(jnp.bfloat16)


def draw_keys(key, part):
    base = jax.random.normal(jax.random.fold_in(key, 3), (TOKENS, KVH * HEAD_DIM), jnp.float32)
    return jnp.clip(base, -8.0, 8.0).astype(jnp.bfloat16)


def draw_selection(key, part):
    ncand = N_SEQ + QB_DEV + SEL
    picks = jax.random.randint(jax.random.fold_in(key, 21), (KVH, N_SEQ, N_SEQ), 0, QB_DEV)
    owner_ids = jnp.arange(N_SEQ, dtype=jnp.int32)
    picks = jnp.where(owner_ids[None, None, :] == 0, 0, picks)
    padded = jnp.concatenate([picks, jnp.zeros((KVH, N_SEQ, QB_DEV + SEL), jnp.int32)], axis=2)[:, :, None, :]
    base = jax.random.randint(jax.random.fold_in(key, 22), (KVH, N_SEQ, QB_DEV, ncand), 0, 4096)
    device = jnp.arange(N_SEQ, dtype=jnp.int32)[None, :, None, None]
    local = jnp.arange(QB_DEV, dtype=jnp.int32)[None, None, :, None]
    cand = jnp.arange(ncand, dtype=jnp.int32)[None, None, None, :]
    remote = cand < N_SEQ
    inner = cand - N_SEQ
    remote_ok = remote & (cand < device)
    local_ok = (cand >= N_SEQ) & (inner <= local)
    usable = remote_ok | local_ok
    block_ids = jnp.where(remote, cand * QB_DEV + padded, device * QB_DEV + inner)
    forced = remote & (cand == 0) & (device > 0) | local_ok & ((inner == local) | (inner == local - 1))
    distance = jnp.where(remote, jnp.minimum(cand, device - 1 - cand), 0)
    weighted = base * 8 // (1 + jnp.maximum(distance, 0))
    weighted = jnp.where(forced, 65536, weighted)
    ranked = jnp.where(usable, weighted * ncand + cand, -1 - cand)
    top, order = lax.top_k(ranked, SEL)
    named = jnp.take_along_axis(block_ids, order, axis=-1)
    named = jnp.where(top >= 0, named, -1)
    return named.transpose(1, 2, 0, 3).reshape(NQB, KVH, SEL).astype(jnp.int32)


def shard_levels(key, extent, cuts, least, high):
    gain, own = 1.0, jax.random.fold_in(key, 6)
    for dim, blocks in cuts:
        draws = jnp.exp(jax.random.uniform(jax.random.fold_in(own, dim), (blocks,), jnp.float32, least / len(cuts), high / len(cuts)))
        gain = gain * jnp.repeat(draws, extent[dim] // blocks).reshape([-1 if axis == dim else 1 for axis in range(len(extent))])
    return gain


def gaussian(own_key, shape, deviation, reach, split=(), kind=jnp.bfloat16):
    factor_of = shard_levels(own_key, shape, split, -0.22, 0.18) if split else 1.0
    array = jax.random.normal(own_key, shape, jnp.float32) * deviation * factor_of
    return jnp.minimum(jnp.maximum(array, -reach), reach).astype(kind)


def setup_inputs(seed: int = 0) -> dict:
    arg_keys = jax.random.split(jax.random.key(seed), 8)
    queries = draw_queries(jax.random.fold_in(arg_keys[7], 71), 0)
    keys = draw_keys(jax.random.fold_in(arg_keys[7], 71), 0)
    values = gaussian(arg_keys[2], (TOKENS, KVH * HEAD_DIM), 1.0, 6.0, ((0, 64), (1, 16)))
    grad_out = gaussian(arg_keys[3], (TOKENS, HEADS * HEAD_DIM), 1.0, 6.0, ((0, 64), (1, 16)))
    gate = jnp.clip(0.05 + 0.9 * jax.random.uniform(arg_keys[4], (TOKENS, HEADS), jnp.float32) ** shard_levels(arg_keys[4], (TOKENS, HEADS), ((0, 64), (1, 16)), -0.2, 0.2), 0.05, 0.95)
    gate_weight = gaussian(arg_keys[5], (HEADS, D), HEADS ** -0.5, 0.75, ((1, 16),))
    selection = draw_selection(jax.random.fold_in(arg_keys[7], 71), 0)
    return {"queries": queries, "keys": keys, "values": values, "grad_out": grad_out, "gate": gate, "gate_weight": gate_weight, "selection": selection}


def rounded(value):
    return lax.optimization_barrier(value.astype(jnp.bfloat16)).astype(jnp.float32)

def reference(queries, keys, values, grad_out, gate, gate_weight, selection):
    scale = 1.0 / math.sqrt(HEAD_DIM)
    key_blocks = keys.reshape(NQB, BLK, KVH, HEAD_DIM).transpose(2, 0, 1, 3)
    value_blocks = values.reshape(NQB, BLK, KVH, HEAD_DIM).transpose(2, 0, 1, 3)
    group_ids = jnp.arange(KVH, dtype=jnp.int32)[:, None]
    offsets = jnp.arange(BLK, dtype=jnp.int32)
    query_tiles = queries.reshape(NQB, BLK, KVH, GQA, HEAD_DIM)
    grad_tiles = grad_out.reshape(NQB, BLK, KVH, GQA, HEAD_DIM)
    gate_tiles = gate.reshape(NQB, BLK, KVH, GQA)

    def step(carry, inputs):
        key_acc, value_acc = carry
        block_index, query_tile, grad_tile, gate_tile, chosen = inputs
        valid = chosen >= 0
        picked = jnp.where(valid, chosen, 0).astype(jnp.int32)
        key_tile = key_blocks[group_ids, picked].astype(jnp.float32)
        value_tile = value_blocks[group_ids, picked].astype(jnp.float32)
        query_f = query_tile.astype(jnp.float32)
        scores = jnp.einsum('tgah,gskh->gatsk', query_f, key_tile) * scale
        key_pos = picked[:, :, None] * BLK + offsets
        query_pos = block_index * BLK + offsets
        allowed = valid[:, None, None, :, None] & (key_pos[:, None, None, :, :] <= query_pos[None, None, :, None, None])
        masked = jnp.where(allowed, scores, -jnp.inf)
        top = lax.optimization_barrier(jnp.max(masked, axis=(3, 4)))
        lse = top + jnp.log(lax.optimization_barrier(jnp.sum(jnp.exp(masked - top[..., None, None]), axis=(3, 4))))
        probs = jnp.exp(masked - lse[..., None, None])
        probs_low = rounded(probs)
        attended = jnp.einsum('gatsk,gskh->tgah', probs_low, value_tile)
        grad_f = grad_tile.astype(jnp.float32)
        grad_att = rounded(gate_tile[..., None] * grad_f)
        gate_sum = lax.optimization_barrier(jnp.sum(grad_f * attended, axis=-1))
        gate_grad = (gate_sum * gate_tile * (1.0 - gate_tile)).astype(jnp.bfloat16)
        delta = lax.optimization_barrier(jnp.sum(grad_att * attended, axis=-1))
        grad_probs = jnp.einsum('tgah,gskh->gatsk', grad_att, value_tile)
        grad_scores = probs * (grad_probs - jnp.transpose(delta, (1, 2, 0))[..., None, None])
        low = rounded(grad_scores)
        grad_query = (jnp.einsum('gatsk,gskh->tgah', low, key_tile) * scale).astype(jnp.bfloat16)
        key_term = jnp.einsum('gatsk,tgah->gskh', low, query_f) * scale
        value_term = jnp.einsum('gatsk,tgah->gskh', probs_low, grad_att)
        key_acc = key_acc.at[group_ids, picked].add(key_term)
        value_acc = value_acc.at[group_ids, picked].add(value_term)
        return ((key_acc, value_acc), (grad_query.reshape(BLK, HEADS * HEAD_DIM), gate_grad.reshape(BLK, HEADS)))
    empty = jnp.zeros((KVH, NQB, BLK, HEAD_DIM), jnp.float32)
    steps_in = (jnp.arange(NQB, dtype=jnp.int32), query_tiles, grad_tiles, gate_tiles, selection)
    (key_acc, value_acc), (grad_queries, gate_grads) = lax.scan(step, (empty, empty), steps_in)
    grad_keys = key_acc.transpose(1, 2, 0, 3).reshape(TOKENS, KVH * HEAD_DIM).astype(jnp.bfloat16)
    grad_values = value_acc.transpose(1, 2, 0, 3).reshape(TOKENS, KVH * HEAD_DIM).astype(jnp.bfloat16)
    gate_all = gate_grads.reshape(TOKENS, HEADS)
    grad_input = jnp.dot(gate_all, gate_weight, preferred_element_type=jnp.float32).astype(jnp.bfloat16)
    return (grad_queries.reshape(TOKENS, HEADS * HEAD_DIM), grad_keys, grad_values, grad_input)
```

```python
import functools
import math

import jax
import jax.numpy as jnp
from jax import lax
from jax.experimental import pallas as pl
from jax.experimental.pallas import tpu as pltpu
from jax.sharding import PartitionSpec as P

BLK = 64
HD = 128
QB = 4
SEL = 16
GQA = 4
NY = 8
NW = 8
NZ = 16
NSEQ = NY * NW
MESH = pl.DeviceIdType.MESH
SCALE = 1.0 / math.sqrt(HD)
EXP2_SCALE = SCALE / math.log(2.0)


def dot(a, b, dims):
    return lax.dot_general(a, b, (dims, ((), ())), preferred_element_type=jnp.float32)


NN = ((1,), (0,))
NT = ((1,), (1,))
TN = ((0,), (0,))


def kernel(
    q_ref, k_ref, v_ref, g_ref, gate_ref, gw_ref, slot_ref, count_ref, pos_ref, req_ref,
    dq_ref, dk_ref, dv_ref, gi_ref,
    col0, col1, col2, col3, col4, col5, col6, col7,
    stage, tab, kc, vc, terms_k, terms_v, gg, gs, gbuf, gwp,
    snd, rx, dn_out, dn_in, up_out, up_in,
    f_s, f_r, b_s, b_r, x_s, x_r, y_s, y_r, dn_s, dn_r, up_s, up_r, g_s, g_r,
):
    cols = (col0, col1, col2, col3, col4, col5, col6, col7)
    s = lax.axis_index("seq")
    z = lax.axis_index("head")
    y = s // NW
    w = lax.rem(s, NW)

    def mate(m):
        return (y * NW + lax.rem(w + m, NW), z)

    def row_of(r):
        return lax.rem(y + (NY - r), NY)

    above = (lax.rem(y + 1, NY) * NW + w, z)
    below = (lax.rem(y + NY - 1, NY) * NW + w, z)

    def zmate(m):
        return (s, lax.rem(z + m, NZ))

    barrier = pltpu.get_barrier_semaphore()
    for m in range(1, NW):
        pl.semaphore_signal(barrier, inc=1, device_id=mate(m), device_id_type=MESH)
    pl.semaphore_signal(barrier, inc=1, device_id=above, device_id_type=MESH)
    pl.semaphore_signal(barrier, inc=1, device_id=below, device_id_type=MESH)
    for m in range(1, NZ):
        pl.semaphore_signal(barrier, inc=1, device_id=zmate(m), device_id_type=MESH)
    own_k = k_ref[...].reshape(QB, BLK, HD)
    own_v = v_ref[...].reshape(QB, BLK, HD)
    cols[0][0] = own_k
    cols[0][1] = own_v
    tab[NSEQ:, 0] = own_k
    tab[NSEQ:, 1] = own_v
    pl.semaphore_wait(barrier, NW + NZ)

    def copy(src, dst, send, recv, to):
        return pltpu.make_async_remote_copy(
            src_ref=src, dst_ref=dst, send_sem=send, recv_sem=recv, device_id=to, device_id_type=MESH
        )

    def ring_up(k):
        return copy(cols[k], cols[k + 1], f_s.at[k], f_r.at[k], above)

    def ring_down(k):
        return copy(cols[(NY - k) % NY], cols[NY - 1 - k], b_s.at[k], b_r.at[k], below)

    def fetch(r, m):
        return copy(stage.at[r, m], tab.at[row_of(r) * NW + w], x_s.at[r, m], x_r.at[r, m], mate(m))

    def arrive(r, m):
        owner = row_of(r) * NW + lax.rem(w + NW - m, NW)
        return copy(stage.at[r, m], tab.at[owner], x_s.at[r, m], x_r.at[r, m], mate(m))

    def hand_out(r):
        owner = row_of(r) * NW + w
        tab[owner] = cols[r][:, jnp.maximum(req_ref[w, owner], 0)]

        def one(m, c):
            block = jnp.maximum(req_ref[lax.rem(w + m, NW), owner], 0)
            stage[r, m] = cols[r][:, block]
            fetch(r, m).start()
            return c

        lax.fori_loop(1, NW, one, 0)

    ring_up(0).start()
    ring_down(0).start()
    hand_out(0)
    for k in range(4):
        ring_up(k).wait_recv()
        if k < 3:
            ring_up(k + 1).start()
        hand_out(k + 1)
        if k < 3:
            ring_down(k).wait_recv()
            if k < 2:
                ring_down(k + 1).start()
            hand_out(NY - 1 - k)

    for r in range(NY):

        def landed(m, c, r=r):
            arrive(r, m).wait_recv()
            return c

        lax.fori_loop(1, NW, landed, 0)

    none = jnp.zeros((BLK, HD), jnp.float32)
    for q in range(QB):
        terms_k[q, SEL] = none
        terms_v[q, SEL] = none

    def attend(q, c):
        rows = pl.ds(pl.multiple_of(q * BLK, BLK), BLK)
        lanes = [slice(h * HD, (h + 1) * HD) for h in range(GQA)]
        qc = jnp.concatenate([q_ref[rows, a] for a in lanes], axis=0)
        gf = jnp.concatenate([g_ref[rows, a] for a in lanes], axis=0).astype(jnp.float32)
        gate = gate_ref[rows, :]
        gate_c = jnp.concatenate(
            [jnp.broadcast_to(gate[:, h : h + 1], (BLK, HD)) for h in range(GQA)], axis=0
        )
        da = (gate_c * gf).astype(jnp.bfloat16)
        for p in range(SEL):
            at = slot_ref[q, p]
            kc[p * BLK : (p + 1) * BLK] = tab[at, 0]
            vc[p * BLK : (p + 1) * BLK] = tab[at, 1]
        keys = kc[...]
        vals = vc[...]
        st = dot(keys, qc, NT)
        u = lax.broadcasted_iota(jnp.int32, (BLK, GQA * BLK), 0)
        t = lax.rem(lax.broadcasted_iota(jnp.int32, (BLK, GQA * BLK), 1), BLK)
        first = jnp.where(u <= t, st[:BLK], -jnp.inf)
        at = lax.broadcasted_iota(jnp.int32, ((SEL - 1) * BLK, GQA * BLK), 0)
        rest = jnp.where(at < (count_ref[q] - 1) * BLK, st[BLK:], -jnp.inf)
        st = jnp.concatenate([first, rest], axis=0)
        top = jnp.max(st, axis=0, keepdims=True)
        e = jnp.exp2((st - top) * EXP2_SCALE)
        probs = e * (1.0 / jnp.sum(e, axis=0, keepdims=True))
        low = probs.astype(jnp.bfloat16)
        att_t = dot(vals, low, TN)
        g_t = gf.T
        gate_t = gate_c.T
        da_t = (gate_t * g_t).astype(jnp.bfloat16).astype(jnp.float32)
        gate_row = gate_t[:1]
        gsum = jnp.sum(g_t * att_t, axis=0, keepdims=True)
        ggrad = (gsum * gate_row * (1.0 - gate_row)).astype(jnp.bfloat16).astype(jnp.float32)
        gg[pl.ds(q, 1), :] = ggrad
        delta = jnp.sum(da_t * att_t, axis=0, keepdims=True)
        dp = dot(vals, da, NT)
        ds = (probs * (dp - delta)).astype(jnp.bfloat16)
        terms_v[q, :SEL] = dot(low, da, NN).reshape(SEL, BLK, HD)
        terms_k[q, :SEL] = (dot(ds, qc, NN) * SCALE).reshape(SEL, BLK, HD)
        dq = (dot(keys, ds, TN) * SCALE).T.astype(jnp.bfloat16)
        for h in range(GQA):
            dq_ref[rows, lanes[h]] = dq[h * BLK : (h + 1) * BLK]
        return c

    lax.fori_loop(0, QB, attend, 0)

    gs[...] = jnp.zeros_like(gs)
    for q in range(QB):
        for h in range(GQA):
            gs[h : h + 1, q * BLK : (q + 1) * BLK] = gg[q : q + 1, h * BLK : (h + 1) * BLK]
    gbuf[z] = gs[...]

    def gate_out(m):
        return copy(gs, gbuf.at[z], g_s.at[m], g_r.at[m], zmate(m))

    def gate_in(m):
        return copy(gs, gbuf.at[lax.rem(z + NZ - m, NZ)], g_s.at[m], g_r.at[m], zmate(m))

    def gate_start(m, c):
        gate_out(m).start()
        return c

    lax.fori_loop(1, NZ, gate_start, 0)

    def give(r, m):
        return copy(snd.at[r, m], rx.at[r, m], y_s.at[r, m], y_r.at[r, m], mate(m))

    def summed(slot):
        total_k = terms_k[0, pos_ref[0, slot]]
        total_v = terms_v[0, pos_ref[0, slot]]
        for q in range(1, QB):
            at = pos_ref[q, slot]
            total_k = total_k + terms_k[q, at]
            total_v = total_v + terms_v[q, at]
        return total_k, total_v

    def send_row(r):
        def one(i, c):
            m = lax.rem(i, NW)
            total_k, total_v = summed(row_of(r) * NW + lax.rem(w + m, NW))
            snd[r, m, 0] = total_k.astype(jnp.bfloat16)
            snd[r, m, 1] = total_v.astype(jnp.bfloat16)

            @pl.when(m > 0)
            def _():
                give(r, m).start()

            return c

        lax.fori_loop(1, NW + 1, one, 0)

    order = (4, 5, 3, 6, 2, 7, 1, 0)
    for r in order:
        send_row(r)

    gwp[...] = jnp.zeros_like(gwp)
    gw = gw_ref[...].astype(jnp.float32)
    for i in range(NZ):
        gwp[8 * i : 8 * i + GQA] = gw[GQA * i : GQA * (i + 1)]

    def reduced(r):
        def wait(m, c):
            give(r, m).wait_recv()
            return c

        lax.fori_loop(1, NW, wait, 0)
        owner = row_of(r) * NW + w
        out = []
        for t in range(2):
            totals = [None] * QB
            for m in range(NW):
                val = (snd[r, 0, t] if m == 0 else rx[r, m, t]).astype(jnp.float32)
                asked = req_ref[lax.rem(w + NW - m, NW), owner]
                for j in range(QB):
                    part = jnp.where(asked == j, val, 0.0)
                    totals[j] = part if m == 0 else totals[j] + part
            out.append(totals)
        return out

    def down(k):
        return copy(dn_out.at[k], dn_in.at[k - 1], dn_s.at[k], dn_r.at[k], below)

    def up(k):
        return copy(up_out.at[k], up_in.at[k - 1], up_s.at[k], up_r.at[k], above)

    for r in order[:-1]:
        if r == 1:
            def gate_wait(m, c):
                gate_in(m).wait_recv()
                return c

            lax.fori_loop(1, NZ, gate_wait, 0)
            gates = gbuf[...].reshape(NZ * 8, QB * BLK).astype(jnp.bfloat16)
            gi_ref[...] = dot(gates, gwp[...].astype(jnp.bfloat16), TN).astype(jnp.bfloat16)
        totals = reduced(r)
        if r <= 4:
            k, inn, out, hop, last = r, dn_in, dn_out, down, 4
        else:
            k, inn, out, hop, last = NY - r, up_in, up_out, up, 3
        if k < last:
            hop(k + 1).wait_recv()
        for t in range(2):
            for j in range(QB):
                val = totals[t][j]
                if k < last:
                    val = val + inn[k, t, j].astype(jnp.float32)
                out[k, t, j] = val.astype(jnp.bfloat16)
        hop(k).start()

    totals = reduced(0)
    down(1).wait_recv()
    up(1).wait_recv()
    for j in range(QB):
        own = summed(NSEQ + j)
        for t, ref in ((0, dk_ref), (1, dv_ref)):
            val = totals[t][j] + own[t]
            val = val + dn_in[0, t, j].astype(jnp.float32) + up_in[0, t, j].astype(jnp.float32)
            ref[j * BLK : (j + 1) * BLK] = val.astype(jnp.bfloat16)

    for k in range(4):
        ring_up(k).wait_send()
        down(k + 1).wait_send()
    for k in range(3):
        ring_down(k).wait_send()
        up(k + 1).wait_send()
    for r in range(NY):

        def sent(m, c, r=r):
            fetch(r, m).wait_send()
            give(r, m).wait_send()
            return c

        lax.fori_loop(1, NW, sent, 0)

    def gate_sent(m, c):
        gate_out(m).wait_send()
        return c

    lax.fori_loop(1, NZ, gate_sent, 0)


def shards(queries, keys, values, grad_out, gate, gate_weight, selection):
    me = lax.axis_index("seq")
    chosen = selection[:, 0, :]
    mine = lax.dynamic_slice_in_dim(chosen, me * QB, QB, 0)
    own = me * QB + jnp.arange(QB, dtype=jnp.int32)[:, None]
    picks = jnp.arange(SEL, dtype=jnp.int32)[None, :]
    ordered = jnp.where(picks == 0, own, jnp.where(mine == own, mine[:, :1], mine))
    valid = ordered >= 0
    owner = ordered // QB
    slot = jnp.where(owner == me, NSEQ + ordered - me * QB, owner)
    slot = jnp.where(valid, slot, NSEQ + own - me * QB)
    count = jnp.sum(valid.astype(jnp.int32), axis=1)
    slots = jnp.arange(NSEQ + QB, dtype=jnp.int32)
    hit = (slot[:, :, None] == slots) & valid[:, :, None]
    pos = jnp.min(jnp.where(hit, picks[:, :, None], SEL), axis=1)
    row = lax.dynamic_slice_in_dim(chosen, me // NW * NW * QB, NW * QB, 0).reshape(NW, QB * SEL)
    owners = jnp.arange(NSEQ, dtype=jnp.int32)
    named = (row // QB)[:, :, None] == owners
    req = jnp.max(jnp.where(named, lax.rem(row, QB)[:, :, None], -1), axis=1)

    vmem = pl.BlockSpec(memory_space=pltpu.VMEM)
    smem = pl.BlockSpec(memory_space=pltpu.SMEM)
    bf, f32 = jnp.bfloat16, jnp.float32
    dma = pltpu.SemaphoreType.DMA
    pair = (2, QB, BLK, HD)
    return pl.pallas_call(
        kernel,
        out_shape=(
            jax.ShapeDtypeStruct(queries.shape, bf),
            jax.ShapeDtypeStruct(keys.shape, bf),
            jax.ShapeDtypeStruct(values.shape, bf),
            jax.ShapeDtypeStruct((queries.shape[0], gate_weight.shape[1]), bf),
        ),
        in_specs=[vmem] * 6 + [smem] * 4,
        out_specs=(vmem,) * 4,
        scratch_shapes=[pltpu.VMEM(pair, bf) for _ in range(NY)]
        + [
            pltpu.VMEM((NY, NW, 2, BLK, HD), bf),
            pltpu.VMEM((NSEQ + QB, 2, BLK, HD), bf),
            pltpu.VMEM((SEL * BLK, HD), bf),
            pltpu.VMEM((SEL * BLK, HD), bf),
            pltpu.VMEM((QB, SEL + 1, BLK, HD), f32),
            pltpu.VMEM((QB, SEL + 1, BLK, HD), f32),
            pltpu.VMEM((8, GQA * BLK), f32),
            pltpu.VMEM((8, QB * BLK), f32),
            pltpu.VMEM((NZ, 8, QB * BLK), f32),
            pltpu.VMEM((NZ * 8, gate_weight.shape[1]), f32),
            pltpu.VMEM((NY, NW, 2, BLK, HD), bf),
            pltpu.VMEM((NY, NW, 2, BLK, HD), bf),
            pltpu.VMEM((5,) + pair, bf),
            pltpu.VMEM((4,) + pair, bf),
            pltpu.VMEM((4,) + pair, bf),
            pltpu.VMEM((3,) + pair, bf),
            dma((4,)), dma((4,)), dma((3,)), dma((3,)),
            dma((NY, NW)), dma((NY, NW)), dma((NY, NW)), dma((NY, NW)),
            dma((5,)), dma((5,)), dma((4,)), dma((4,)),
            dma((NZ,)), dma((NZ,)),
        ],
        compiler_params=pltpu.CompilerParams(
            collective_id=0, has_side_effects=True, vmem_limit_bytes=56 << 20
        ),
    )(queries, keys, values, grad_out, gate, gate_weight, slot, count, pos, req)


def solution(mesh):
    placed = (
        P("seq", "head"),
        P("seq", "head"),
        P("seq", "head"),
        P("seq", "head"),
        P("seq", "head"),
        P(None, "head"),
        P(None, "head", None),
    )
    return jax.shard_map(
        shards,
        mesh=mesh,
        in_specs=placed,
        out_specs=(P("seq", "head"), P("seq", "head"), P("seq", "head"), P("seq", "head")),
        check_vma=False,
    )
```

```python
import functools
import math

import jax
import jax.numpy as jnp
from jax import lax
from jax.experimental import pallas as pl
from jax.experimental.pallas import tpu as pltpu
from jax.sharding import PartitionSpec as P

BLK = 64
HD = 128
QB = 4
SEL = 16
GQA = 4
NY = 8
NW = 8
NZ = 16
NSEQ = NY * NW
MESH = pl.DeviceIdType.MESH
SCALE = 1.0 / math.sqrt(HD)
EXP2_SCALE = SCALE / math.log(2.0)


def dot(a, b, dims):
    return lax.dot_general(a, b, (dims, ((), ())), preferred_element_type=jnp.float32)


NN = ((1,), (0,))
NT = ((1,), (1,))
TN = ((0,), (0,))


def kernel(
    q_hbm, k_hbm, v_hbm, g_hbm, gate_hbm, gw_hbm, sel_hbm,
    dq_hbm, dk_ref, dv_ref, gi_hbm,
    *scratch,
):
    cols = (scratch[:NY], scratch[NY : 2 * NY])
    (
        q_ref, g_ref, gate_ref, gw_ref, sel_ref, dq_ref, gi_ref,
        tbl, req_s, code_s, pos_s,
        stage, tab_k, tab_v, kc, vc, probs_ref, qc_ref, da_ref, terms_k, terms_v,
        gr, gg, gbuf, gwp, snd, rx, dn_out, dn_in, up_out, up_in,
        in_s, out_s, t_s, f_s, f_r, b_s, b_r, x_s, x_r, y_s, y_r, dn_s, dn_r, up_s, up_r, gu_s, gu_r, gd_s, gd_r,
    ) = scratch[2 * NY :]
    tab = (tab_k, tab_v)
    terms = (terms_k, terms_v)
    s = lax.axis_index("seq")
    z = lax.axis_index("head")
    y = s // NW
    w = lax.rem(s, NW)

    def mate(m):
        return (y * NW + lax.rem(w + m, NW), z)

    def row_of(r):
        return lax.rem(y + (NY - r), NY)

    above = (lax.rem(y + 1, NY) * NW + w, z)
    below = (lax.rem(y + NY - 1, NY) * NW + w, z)
    ahead = [(s, lax.rem(z + i, NZ)) for i in (1, 2)]
    behind = [(s, lax.rem(z + NZ - i, NZ)) for i in (1, 2)]

    barrier = pltpu.get_barrier_semaphore()
    for m in range(1, NW):
        pl.semaphore_signal(barrier, inc=1, device_id=mate(m), device_id_type=MESH)
    for to in (above, below, *ahead, *behind):
        pl.semaphore_signal(barrier, inc=1, device_id=to, device_id_type=MESH)

    loads = [
        pltpu.make_async_copy(a, b, in_s.at[i])
        for i, (a, b) in enumerate(
            (
                (k_hbm, cols[0][0]), (v_hbm, cols[1][0]), (sel_hbm, sel_ref),
                (k_hbm, tab_k.at[pl.ds(NSEQ, QB)]), (v_hbm, tab_v.at[pl.ds(NSEQ, QB)]),
                (gate_hbm, gate_ref), (g_hbm, g_ref), (q_hbm, q_ref), (gw_hbm, gw_ref),
            )
        )
    ]
    for load in loads:
        load.start()

    loads[2].wait()
    sel = sel_ref[...]
    owner = jnp.right_shift(sel, 2)
    inner = jnp.bitwise_and(sel, 3)
    code = jnp.where(owner == s, NSEQ + inner, owner)
    mine = lax.broadcasted_iota(jnp.int32, (NY, NSEQ * QB), 0) * NW + w
    slots = lax.broadcasted_iota(jnp.int32, (NSEQ + 8, NSEQ * QB), 0)
    req = jnp.full((NY, NSEQ * QB), -1, jnp.int32)
    for p in range(SEL):
        req = jnp.where(owner[p : p + 1] == mine, inner[p : p + 1], req)
    tbl[0:NY] = req
    half = pl.ds(pl.multiple_of(y // 4 * HD, HD), HD)
    req_in = pltpu.make_async_copy(tbl.at[pl.ds(0, NY), half], req_s, t_s.at[0])
    req_in.start()
    pos = jnp.full((NSEQ + 8, NSEQ * QB), SEL, jnp.int32)
    for p in range(SEL):
        pos = jnp.where(code[p : p + 1] == slots, p, pos)
    tbl[NY : NY + SEL] = code
    tbl[NY + SEL :] = pos
    code_in = pltpu.make_async_copy(tbl.at[pl.ds(NY, SEL), half], code_s, t_s.at[1])
    pos_in = pltpu.make_async_copy(tbl.at[pl.ds(NY + SEL, NSEQ + 8), half], pos_s, t_s.at[2])
    code_in.start()
    pos_in.start()
    row_lane = lax.rem(y, 4) * (NW * QB)
    lane = row_lane + w * QB

    def asked(r, d):
        at = row_lane + d * QB
        got = req_s[row_of(r), at]
        for q in range(1, QB):
            got = jnp.maximum(got, req_s[row_of(r), at + q])
        return got

    loads[0].wait()
    loads[1].wait()
    pl.semaphore_wait(barrier, NW + 5)

    def copy(src, dst, send, recv, to):
        return pltpu.make_async_remote_copy(
            src_ref=src, dst_ref=dst, send_sem=send, recv_sem=recv, device_id=to, device_id_type=MESH
        )

    def ring_up(t, k):
        return copy(cols[t][k], cols[t][k + 1], f_s.at[t, k], f_r.at[t, k], above)

    def ring_down(t, k):
        return copy(cols[t][(NY - k) % NY], cols[t][NY - 1 - k], b_s.at[t, k], b_r.at[t, k], below)

    def fetch(t, r, m):
        return copy(stage.at[t, r, m], tab[t].at[row_of(r) * NW + w], x_s.at[t, r, m], x_r.at[t, r, m], mate(m))

    def arrive(t, r, m):
        home = row_of(r) * NW + lax.rem(w + NW - m, NW)
        return copy(stage.at[t, r, m], tab[t].at[home], x_s.at[t, r, m], x_r.at[t, r, m], mate(m))

    def hand_out(t, r):
        tab[t][row_of(r) * NW + w] = cols[t][r][jnp.maximum(asked(r, w), 0)]

        def one(m, c):
            block = jnp.maximum(asked(r, lax.rem(w + m, NW)), 0)
            stage[t, r, m] = cols[t][r][block]
            fetch(t, r, m).start()
            return c

        lax.fori_loop(1, NW, one, 0)

    for t in range(2):
        ring_up(t, 0).start()
        ring_down(t, 0).start()
    req_in.wait()
    hand_out(0, 0)
    hand_out(1, 0)
    for k in range(4):
        for t in range(2):
            ring_up(t, k).wait_recv()
            if k < 3:
                ring_up(t, k + 1).start()
                if t == 0:
                    hand_out(0, k + 1)
                ring_down(t, k).wait_recv()
                if k < 2:
                    ring_down(t, k + 1).start()
                if t == 0:
                    hand_out(0, NY - 1 - k)
            elif t == 0:
                hand_out(0, 4)
        if k > 0:
            hand_out(1, k)
            hand_out(1, NY - k)
    hand_out(1, 4)

    none = jnp.zeros((BLK, HD), jnp.float32)
    for q in range(QB):
        terms_k[q, SEL] = none
        terms_v[q, SEL] = none
    for load in loads[3:]:
        load.wait()
    for q in range(QB):
        for h in range(GQA):
            gr[q : q + 1, h * BLK : (h + 1) * BLK] = gate_ref[h : h + 1, q * BLK : (q + 1) * BLK]
    gwp[...] = jnp.zeros_like(gwp)
    gw = gw_ref[...].astype(jnp.float32)
    for i in range(NZ):
        gwp[8 * i : 8 * i + GQA] = gw[GQA * i : GQA * (i + 1)]
    code_in.wait()
    pos_in.wait()

    def all_in(t):
        for r in range(NY):

            def landed(m, c, r=r):
                arrive(t, r, m).wait_recv()
                return c

            lax.fori_loop(1, NW, landed, 0)

    lanes = [slice(h * HD, (h + 1) * HD) for h in range(GQA)]
    below_diag = lax.broadcasted_iota(jnp.int32, (BLK, GQA * BLK), 0) - lax.rem(
        lax.broadcasted_iota(jnp.int32, (BLK, GQA * BLK), 1), BLK
    )

    def gather(t, q, p):
        at = code_s[p, lane + q]
        return tab[t][jnp.where(at < 0, NSEQ, at)]

    def gate_of(q):
        row = gr[pl.ds(q, 1), :]
        return row, jnp.broadcast_to(row, (HD, GQA * BLK))

    def score(q, c):
        rows = pl.ds(pl.multiple_of(q * BLK, BLK), BLK)
        qc = jnp.concatenate([q_ref[rows, a] for a in lanes], axis=0)
        gf = jnp.concatenate([g_ref[rows, a] for a in lanes], axis=0).astype(jnp.float32)
        da = (gate_of(q)[1].T * gf).astype(jnp.bfloat16)
        qc_ref[q] = qc
        da_ref[q] = da
        for p in range(SEL):
            kc[q, p * BLK : (p + 1) * BLK] = gather(0, q, p)
        st = dot(kc[q], qc, NT)
        parts = []
        for p in range(SEL):
            at = code_s[p, lane + q]
            reach = jnp.where(at == NSEQ + q, 0, jnp.where(at < 0, -BLK, BLK))
            parts.append(jnp.where(below_diag <= reach, st[p * BLK : (p + 1) * BLK], -jnp.inf))
        st = jnp.concatenate(parts, axis=0)
        top = jnp.max(st, axis=0, keepdims=True)
        e = jnp.exp2((st - top) * EXP2_SCALE)
        probs = e * (1.0 / jnp.sum(e, axis=0, keepdims=True))
        probs_ref[q] = probs
        terms_v[q, :SEL] = dot(probs.astype(jnp.bfloat16), da, NN).reshape(SEL, BLK, HD)
        return c

    def attend(q, c):
        rows = pl.ds(pl.multiple_of(q * BLK, BLK), BLK)
        for p in range(SEL):
            vc[p * BLK : (p + 1) * BLK] = gather(1, q, p)
        vals = vc[...]
        probs = probs_ref[q]
        qc = qc_ref[q]
        da = da_ref[q]
        att_t = dot(vals, probs.astype(jnp.bfloat16), TN)
        g_t = jnp.concatenate([g_ref[rows, a] for a in lanes], axis=0).astype(jnp.float32).T
        gate_row, gate_t = gate_of(q)
        da_t = (gate_t * g_t).astype(jnp.bfloat16).astype(jnp.float32)
        gsum = jnp.sum(g_t * att_t, axis=0, keepdims=True)
        ggrad = (gsum * gate_row * (1.0 - gate_row)).astype(jnp.bfloat16).astype(jnp.float32)
        gg[pl.ds(q, 1), :] = ggrad
        delta = jnp.sum(da_t * att_t, axis=0, keepdims=True)
        dp = dot(vals, da, NT)
        ds = (probs * (dp - delta)).astype(jnp.bfloat16)
        terms_k[q, :SEL] = (dot(ds, qc, NN) * SCALE).reshape(SEL, BLK, HD)
        dq = (dot(kc[q], ds, TN) * SCALE).T.astype(jnp.bfloat16)
        for h in range(GQA):
            dq_ref[rows, lanes[h]] = dq[h * BLK : (h + 1) * BLK]
        return c

    def give(t, r, m):
        return copy(snd.at[t, r, m], rx.at[t, r, m], y_s.at[t, r, m], y_r.at[t, r, m], mate(m))

    def summed(t, slot):
        total = terms[t][0, pos_s[slot, lane]]
        for q in range(1, QB):
            total = total + terms[t][q, pos_s[slot, lane + q]]
        return total

    def send_row(t, r):
        def one(i, c):
            m = lax.rem(i, NW)
            snd[t, r, m] = summed(t, row_of(r) * NW + lax.rem(w + m, NW)).astype(jnp.bfloat16)

            @pl.when(m > 0)
            def _():
                give(t, r, m).start()

            return c

        lax.fori_loop(1, NW + 1, one, 0)

    order = (4, 5, 3, 6, 2, 7, 1, 0)

    all_in(0)
    lax.fori_loop(0, QB, score, 0)
    for r in order:
        send_row(1, r)
    all_in(1)
    lax.fori_loop(0, QB, attend, 0)
    for r in order:
        send_row(0, r)
    dq_out = pltpu.make_async_copy(dq_ref, dq_hbm, out_s.at[0])
    dq_out.start()

    gbuf[z] = jnp.zeros((8, QB * BLK), jnp.float32)
    for q in range(QB):
        for h in range(GQA):
            gbuf[z, h : h + 1, q * BLK : (q + 1) * BLK] = gg[q : q + 1, h * BLK : (h + 1) * BLK]

    def gate_up(d):
        at = gbuf.at[lax.rem(z + NZ - max(d - 2, 0), NZ)]
        return copy(at, at, gu_s.at[d - 1], gu_r.at[d - 1], ahead[min(d, 2) - 1])

    def gate_up_in(d):
        at = gbuf.at[lax.rem(z + NZ - d, NZ)]
        return copy(at, at, gu_s.at[d - 1], gu_r.at[d - 1], ahead[min(d, 2) - 1])

    def gate_down(d):
        at = gbuf.at[lax.rem(z + max(d - 2, 0), NZ)]
        return copy(at, at, gd_s.at[d - 1], gd_r.at[d - 1], behind[min(d, 2) - 1])

    def gate_down_in(d):
        at = gbuf.at[lax.rem(z + d, NZ)]
        return copy(at, at, gd_s.at[d - 1], gd_r.at[d - 1], behind[min(d, 2) - 1])

    for d in (1, 2):
        gate_up(d).start()
        gate_down(d).start()

    def gate_step(k):
        for d in (2 * k - 1, 2 * k):
            gate_up_in(d).wait_recv()
            if d + 2 <= 8:
                gate_up(d + 2).start()
            if d <= 7:
                gate_down_in(d).wait_recv()
                if d + 2 <= 7:
                    gate_down(d + 2).start()

    def reduced(t, r):
        def wait(m, c):
            give(t, r, m).wait_recv()
            return c

        lax.fori_loop(1, NW, wait, 0)
        totals = [None] * QB
        for m in range(NW):
            val = (snd[t, r, 0] if m == 0 else rx[t, r, m]).astype(jnp.float32)
            which = asked(r, lax.rem(w + NW - m, NW))
            for j in range(QB):
                part = jnp.where(which == j, val, 0.0)
                totals[j] = part if m == 0 else totals[j] + part
        return totals

    def down(t, k):
        return copy(dn_out.at[t, k], dn_in.at[t, k - 1], dn_s.at[t, k], dn_r.at[t, k], below)

    def up(t, k):
        return copy(up_out.at[t, k], up_in.at[t, k - 1], up_s.at[t, k], up_r.at[t, k], above)

    def pass_on(t, r):
        totals = reduced(t, r)
        if r <= 4:
            k, inn, out, hop, last = r, dn_in, dn_out, down, 4
        else:
            k, inn, out, hop, last = NY - r, up_in, up_out, up, 3
        if k < last:
            hop(t, k + 1).wait_recv()
        for j in range(QB):
            val = totals[j]
            if k < last:
                val = val + inn[t, k, j].astype(jnp.float32)
            out[t, k, j] = val.astype(jnp.bfloat16)
        hop(t, k).start()

    def finish(t, ref):
        totals = reduced(t, 0)
        down(t, 1).wait_recv()
        up(t, 1).wait_recv()
        for j in range(QB):
            val = totals[j] + summed(t, NSEQ + j)
            val = val + dn_in[t, 0, j].astype(jnp.float32) + up_in[t, 0, j].astype(jnp.float32)
            ref[j] = val.astype(jnp.bfloat16)

    pass_on(1, 4)
    pass_on(1, 5)
    pass_on(1, 3)
    gate_step(1)
    pass_on(1, 6)
    pass_on(0, 4)
    pass_on(0, 5)
    pass_on(1, 2)
    gate_step(2)
    pass_on(1, 7)
    pass_on(0, 3)
    pass_on(0, 6)
    pass_on(1, 1)
    gate_step(3)
    pass_on(0, 2)
    pass_on(0, 7)
    finish(1, dv_ref)
    gate_step(4)
    pass_on(0, 1)
    gates = gbuf[...].reshape(NZ * 8, QB * BLK).astype(jnp.bfloat16)
    gi_ref[...] = dot(gwp[...].astype(jnp.bfloat16), gates, TN).astype(jnp.bfloat16)
    gi_out = pltpu.make_async_copy(gi_ref, gi_hbm, out_s.at[1])
    gi_out.start()
    finish(0, dk_ref)

    for t in range(2):
        for k in range(4):
            ring_up(t, k).wait_send()
            down(t, k + 1).wait_send()
        for k in range(3):
            ring_down(t, k).wait_send()
            up(t, k + 1).wait_send()
        for r in range(NY):

            def sent(m, c, t=t, r=r):
                fetch(t, r, m).wait_send()
                give(t, r, m).wait_send()
                return c

            lax.fori_loop(1, NW, sent, 0)
    for d in range(1, 9):
        gate_up(d).wait_send()
        if d < 8:
            gate_down(d).wait_send()
    dq_out.wait()
    gi_out.wait()


def place(*refs):
    half = len(refs) // 2
    for src, dst in zip(refs[:half], refs[half:]):
        dst[...] = src[...]


def shards(queries, keys, values, grad_out, gate, gate_weight, selection):
    vmem = pl.BlockSpec(memory_space=pltpu.VMEM)
    hbm = pl.BlockSpec(memory_space=pl.ANY)
    bf, f32, i32 = jnp.bfloat16, jnp.float32, jnp.int32
    dma = pltpu.SemaphoreType.DMA
    blocks = (QB, BLK, HD)
    tokens, width = queries.shape
    depth = gate_weight.shape[1]
    outs = (
        jax.ShapeDtypeStruct(queries.shape, bf),
        jax.ShapeDtypeStruct(blocks, bf),
        jax.ShapeDtypeStruct(blocks, bf),
        jax.ShapeDtypeStruct((depth, tokens), bf),
    )
    results = pl.pallas_call(
        kernel,
        out_shape=outs,
        in_specs=[hbm] * 7,
        out_specs=(hbm, vmem, vmem, hbm),
        scratch_shapes=[pltpu.VMEM(blocks, bf) for _ in range(2 * NY)]
        + [
            pltpu.VMEM((tokens, width), bf),
            pltpu.VMEM((tokens, width), bf),
            pltpu.VMEM((GQA, tokens), f32),
            pltpu.VMEM((NZ * GQA, depth), bf),
            pltpu.VMEM((SEL, NSEQ * QB), i32),
            pltpu.VMEM((tokens, width), bf),
            pltpu.VMEM((depth, tokens), bf),
            pltpu.VMEM((NY + SEL + NSEQ + 8, NSEQ * QB), i32),
            pltpu.SMEM((NY, HD), i32),
            pltpu.SMEM((SEL, HD), i32),
            pltpu.SMEM((NSEQ + 8, HD), i32),
            pltpu.VMEM((2, NY, NW, BLK, HD), bf),
            pltpu.VMEM((NSEQ + QB, BLK, HD), bf),
            pltpu.VMEM((NSEQ + QB, BLK, HD), bf),
            pltpu.VMEM((QB, SEL * BLK, HD), bf),
            pltpu.VMEM((SEL * BLK, HD), bf),
            pltpu.VMEM((QB, SEL * BLK, GQA * BLK), f32),
            pltpu.VMEM((QB, GQA * BLK, HD), bf),
            pltpu.VMEM((QB, GQA * BLK, HD), bf),
            pltpu.VMEM((QB, SEL + 1, BLK, HD), f32),
            pltpu.VMEM((QB, SEL + 1, BLK, HD), f32),
            pltpu.VMEM((8, GQA * BLK), f32),
            pltpu.VMEM((8, GQA * BLK), f32),
            pltpu.VMEM((NZ, 8, QB * BLK), f32),
            pltpu.VMEM((NZ * 8, depth), f32),
            pltpu.VMEM((2, NY, NW, BLK, HD), bf),
            pltpu.VMEM((2, NY, NW, BLK, HD), bf),
            pltpu.VMEM((2, 5) + blocks, bf),
            pltpu.VMEM((2, 4) + blocks, bf),
            pltpu.VMEM((2, 4) + blocks, bf),
            pltpu.VMEM((2, 3) + blocks, bf),
            dma((9,)), dma((2,)), dma((3,)),
            dma((2, 4)), dma((2, 4)), dma((2, 3)), dma((2, 3)),
            dma((2, NY, NW)), dma((2, NY, NW)), dma((2, NY, NW)), dma((2, NY, NW)),
            dma((2, 5)), dma((2, 5)), dma((2, 4)), dma((2, 4)),
            dma((8,)), dma((8,)), dma((7,)), dma((7,)),
        ],
        compiler_params=pltpu.CompilerParams(
            collective_id=0, has_side_effects=True, vmem_limit_bytes=56 << 20
        ),
    )(
        queries,
        keys.reshape(blocks),
        values.reshape(blocks),
        grad_out,
        gate.T,
        gate_weight,
        selection.transpose(1, 2, 0)[0],
    )
    dq, dk, dv, gi = pl.pallas_call(
        place,
        out_shape=outs,
        in_specs=[vmem] * 4,
        out_specs=(vmem,) * 4,
        compiler_params=pltpu.CompilerParams(vmem_limit_bytes=56 << 20),
    )(*results)
    return dq, dk.reshape(keys.shape), dv.reshape(values.shape), gi.T


def solution(mesh):
    placed = (
        P("seq", "head"),
        P("seq", "head"),
        P("seq", "head"),
        P("seq", "head"),
        P("seq", "head"),
        P(None, "head"),
        P(None, "head", None),
    )
    return jax.shard_map(
        shards,
        mesh=mesh,
        in_specs=placed,
        out_specs=(P("seq", "head"), P("seq", "head"), P("seq", "head"), P("seq", "head")),
        check_vma=False,
    )
```

```python
import functools
import math

import jax
import jax.numpy as jnp
from jax import lax
from jax.experimental import pallas as pl
from jax.experimental.pallas import tpu as pltpu
from jax.sharding import PartitionSpec as P

BLK = 64
HD = 128
QB = 4
SEL = 16
GQA = 4
NY = 8
NW = 8
NZ = 16
NSEQ = NY * NW
REACH = 6
CUTS = 4
MESH = pl.DeviceIdType.MESH
SCALE = 1.0 / math.sqrt(HD)
EXP2_SCALE = SCALE / math.log(2.0)


def dot(a, b, dims):
    return lax.dot_general(a, b, (dims, ((), ())), preferred_element_type=jnp.float32)


NN = ((1,), (0,))
NT = ((1,), (1,))
TN = ((0,), (0,))


def kernel(
    q_hbm, k_hbm, v_hbm, g_hbm, gate_hbm, gw_hbm, sel_hbm,
    dq_hbm, dk_ref, dv_ref, gi_hbm,
    *scratch,
):
    cols = (scratch[:REACH], scratch[REACH : 2 * REACH])
    (
        q_ref, g_ref, gate_ref, gw_ref, sel_ref, dq_ref, gi_ref,
        ds_ref, tbl, req_s, code_s, pos_s,
        stage, tab_k, tab_v, kc, vc, probs_ref, qc_ref, da_ref, terms_k, terms_v,
        gr, gg, gbuf, gwp, snd, rx, sum_out, sum_in, fin,
        far_stage, far_tab, far_snd, far_rx, far_in,
        in_s, out_s, t_s, f_s, f_r, x_s, x_r, y_s, y_r, d_s, d_r, gu_s, gu_r, gd_s, gd_r,
        fx_s, fx_r, fy_s, fy_r, by_s, by_r, bx_s, bx_r,
    ) = scratch[2 * REACH :]
    tab = (tab_k, tab_v)
    terms = (terms_k, terms_v)
    s = lax.axis_index("seq")
    z = lax.axis_index("head")
    y = s // NW
    w = lax.rem(s, NW)

    def mate(m):
        return (y * NW + lax.rem(w + m, NW), z)

    def row_of(r):
        return lax.rem(y + (NY - r), NY)

    def up_by(n):
        return (lax.rem(y + n + NY, NY) * NW + w, z)

    ahead = [(s, lax.rem(z + i, NZ)) for i in (1, 2)]
    behind = [(s, lax.rem(z + NZ - i, NZ)) for i in (1, 2)]

    barrier = pltpu.get_barrier_semaphore()
    for m in range(1, NW):
        pl.semaphore_signal(barrier, inc=1, device_id=mate(m), device_id_type=MESH)
    for to in (up_by(1), up_by(-1), up_by(2), up_by(-2), *ahead, *behind):
        pl.semaphore_signal(barrier, inc=1, device_id=to, device_id_type=MESH)

    loads = [
        pltpu.make_async_copy(a, b, in_s.at[i])
        for i, (a, b) in enumerate(
            (
                (k_hbm, cols[0][0]), (v_hbm, cols[1][0]), (sel_hbm, sel_ref),
                (k_hbm, tab_k.at[pl.ds(NSEQ, QB)]), (v_hbm, tab_v.at[pl.ds(NSEQ, QB)]),
                (gate_hbm, gate_ref), (g_hbm, g_ref), (q_hbm, q_ref), (gw_hbm, gw_ref),
            )
        )
    ]
    for load in loads:
        load.start()

    loads[2].wait()
    sel = sel_ref[...]
    owner = jnp.right_shift(sel, 2)
    inner = jnp.bitwise_and(sel, 3)
    code = jnp.where(owner == s, NSEQ + inner, owner)
    mine = lax.broadcasted_iota(jnp.int32, (NY, NSEQ * QB), 0) * NW + w
    slots = lax.broadcasted_iota(jnp.int32, (NSEQ + 8, NSEQ * QB), 0)
    req = jnp.full((NY, NSEQ * QB), -1, jnp.int32)
    for p in range(SEL):
        req = jnp.where(owner[p : p + 1] == mine, inner[p : p + 1], req)
    tbl[0:NY] = req
    half = pl.ds(pl.multiple_of(y // 4 * HD, HD), HD)
    req_in = pltpu.make_async_copy(tbl.at[pl.ds(0, NY)], req_s, t_s.at[0])
    req_in.start()
    pos = jnp.full((NSEQ + 8, NSEQ * QB), SEL, jnp.int32)
    for p in range(SEL):
        pos = jnp.where(code[p : p + 1] == slots, p, pos)
    tbl[NY : NY + SEL] = code
    tbl[NY + SEL :] = pos
    code_in = pltpu.make_async_copy(tbl.at[pl.ds(NY, SEL), half], code_s, t_s.at[1])
    pos_in = pltpu.make_async_copy(tbl.at[pl.ds(NY + SEL, NSEQ + 8), half], pos_s, t_s.at[2])
    code_in.start()
    pos_in.start()
    lane = lax.rem(s * QB, HD)

    def asked(row, d):
        got = req_s[row, d * QB]
        for q in range(1, QB):
            got = jnp.maximum(got, req_s[row, d * QB + q])
        return got

    loads[0].wait()
    loads[1].wait()
    pl.semaphore_wait(barrier, NW + 7)

    def copy(src, dst, send, recv, to):
        return pltpu.make_async_remote_copy(
            src_ref=src, dst_ref=dst, send_sem=send, recv_sem=recv, device_id=to, device_id_type=MESH
        )

    def spread(t, r, c):
        part = pl.ds(c * (QB // CUTS), QB // CUTS)
        return copy(
            cols[t][r - 1].at[part], cols[t][r].at[part], f_s.at[t, r, c], f_r.at[t, r, c], up_by(1)
        )

    def spread_start(t, r, c):
        @pl.when((y >= r - 1) & (y < NY - 1))
        def _():
            spread(t, r, c).start()

    def spread_in(t, r, c):
        @pl.when(y >= r)
        def _():
            spread(t, r, c).wait_recv()

    def fetch(t, r, m):
        return copy(stage.at[t, r, m], tab[t].at[row_of(r) * NW + w], x_s.at[t, r, m], x_r.at[t, r, m], mate(m))

    def arrive(t, r, m):
        home = row_of(r) * NW + lax.rem(w + NW - m, NW)
        return copy(stage.at[t, r, m], tab[t].at[home], x_s.at[t, r, m], x_r.at[t, r, m], mate(m))

    def hand_out(t, r):
        @pl.when(y >= r)
        def _():
            row = row_of(r)
            tab[t][row * NW + w] = cols[t][r][jnp.maximum(asked(row, s), 0)]

            def one(m, c):
                block = jnp.maximum(asked(row, y * NW + lax.rem(w + m, NW)), 0)
                stage[t, r, m] = cols[t][r][block]
                fetch(t, r, m).start()
                return c

            lax.fori_loop(1, NW, one, 0)

    def far_row(j):
        return NY - 1 - j

    def far_fetch(t, j, m):
        return copy(far_stage.at[t, j, m], far_tab.at[t, j, w], fx_s.at[t, j, m], fx_r.at[t, j, m], mate(m))

    def far_arrive(t, j, m):
        at = lax.rem(w + NW - m, NW)
        return copy(far_stage.at[t, j, m], far_tab.at[t, j, at], fx_s.at[t, j, m], fx_r.at[t, j, m], mate(m))

    def far_push(t, j):
        return copy(
            far_tab.at[t, j], tab[t].at[pl.ds(y * NW, NW)], fy_s.at[t, j], fy_r.at[t, y], (far_row(j) * NW + w, z)
        )

    def far_landed(t, o):
        return copy(far_tab.at[t, 0], tab[t].at[pl.ds(o * NW, NW)], fy_s.at[t, 0], fy_r.at[t, o], up_by(1))

    def far_hand_out(t):
        for j in range(2):

            @pl.when(y < 2 - j)
            def _(j=j):
                far_tab[t, j, w] = cols[t][0][jnp.maximum(asked(y, far_row(j) * NW + w), 0)]

                def one(m, c):
                    block = jnp.maximum(asked(y, far_row(j) * NW + lax.rem(w + m, NW)), 0)
                    far_stage[t, j, m] = cols[t][0][block]
                    far_fetch(t, j, m).start()
                    return c

                lax.fori_loop(1, NW, one, 0)

    def far_forward(t):
        for j in range(2):

            @pl.when(y < 2 - j)
            def _(j=j):
                def landed(m, c):
                    far_arrive(t, j, m).wait_recv()
                    return c

                lax.fori_loop(1, NW, landed, 0)
                far_push(t, j).start()

    for c in range(CUTS):
        for t in range(2):
            spread_start(t, 1, c)
    req_in.wait()
    for t in range(2):
        hand_out(t, 0)
        far_hand_out(t)
    for k in range(1, REACH + 1):
        if k < REACH:
            for c in range(CUTS):
                spread_in(0, k, c)
                if k < REACH - 1:
                    spread_start(0, k + 1, c)
            hand_out(0, k)
        if k > 1:
            for c in range(CUTS):
                spread_in(1, k - 1, c)
                if k < REACH:
                    spread_start(1, k, c)
            hand_out(1, k - 1)
        if k < 3:
            far_forward(k - 1)

    none = jnp.zeros((BLK, HD), jnp.float32)
    for q in range(QB):
        terms_k[q, SEL] = none
        terms_v[q, SEL] = none
    for load in loads[3:]:
        load.wait()
    for q in range(QB):
        for h in range(GQA):
            gr[q : q + 1, h * BLK : (h + 1) * BLK] = gate_ref[h : h + 1, q * BLK : (q + 1) * BLK]
    gwp[...] = jnp.zeros_like(gwp)
    gw = gw_ref[...].astype(jnp.float32)
    for i in range(NZ):
        gwp[8 * i : 8 * i + GQA] = gw[GQA * i : GQA * (i + 1)]
    code_in.wait()
    pos_in.wait()

    def all_in(t):
        for r in range(REACH):

            @pl.when(y >= r)
            def _(r=r):
                def landed(m, c):
                    arrive(t, r, m).wait_recv()
                    return c

                lax.fori_loop(1, NW, landed, 0)

        for o in range(2):

            @pl.when(y >= NY - 2 + o)
            def _(o=o):
                far_landed(t, o).wait_recv()

    lanes = [slice(h * HD, (h + 1) * HD) for h in range(GQA)]
    below_diag = lax.broadcasted_iota(jnp.int32, (BLK, GQA * BLK), 0) - lax.rem(
        lax.broadcasted_iota(jnp.int32, (BLK, GQA * BLK), 1), BLK
    )

    def gather(t, q, p):
        at = code_s[p, lane + q]
        return tab[t][jnp.where(at < 0, NSEQ, at)]

    def gate_of(q):
        row = gr[pl.ds(q, 1), :]
        return row, jnp.broadcast_to(row, (HD, GQA * BLK))

    def score(q, c):
        rows = pl.ds(pl.multiple_of(q * BLK, BLK), BLK)
        qc = jnp.concatenate([q_ref[rows, a] for a in lanes], axis=0)
        gf = jnp.concatenate([g_ref[rows, a] for a in lanes], axis=0).astype(jnp.float32)
        da = (gate_of(q)[1].T * gf).astype(jnp.bfloat16)
        qc_ref[q] = qc
        da_ref[q] = da
        for p in range(SEL):
            kc[q, p * BLK : (p + 1) * BLK] = gather(0, q, p)
        st = dot(kc[q], qc, NT)
        parts = []
        for p in range(SEL):
            at = code_s[p, lane + q]
            reach = jnp.where(at == NSEQ + q, 0, jnp.where(at < 0, -BLK, BLK))
            parts.append(jnp.where(below_diag <= reach, st[p * BLK : (p + 1) * BLK], -jnp.inf))
        st = jnp.concatenate(parts, axis=0)
        top = jnp.max(st, axis=0, keepdims=True)
        e = jnp.exp2((st - top) * EXP2_SCALE)
        probs = e * (1.0 / jnp.sum(e, axis=0, keepdims=True))
        probs_ref[q] = probs
        terms_v[q, :SEL] = dot(probs.astype(jnp.bfloat16), da, NN).reshape(SEL, BLK, HD)
        return c

    def attend(q, c):
        rows = pl.ds(pl.multiple_of(q * BLK, BLK), BLK)
        for p in range(SEL):
            vc[p * BLK : (p + 1) * BLK] = gather(1, q, p)
        vals = vc[...]
        probs = probs_ref[q]
        qc = qc_ref[q]
        da = da_ref[q]
        att_t = dot(vals, probs.astype(jnp.bfloat16), TN)
        g_t = jnp.concatenate([g_ref[rows, a] for a in lanes], axis=0).astype(jnp.float32).T
        gate_row, gate_t = gate_of(q)
        da_t = (gate_t * g_t).astype(jnp.bfloat16).astype(jnp.float32)
        gsum = jnp.sum(g_t * att_t, axis=0, keepdims=True)
        ggrad = (gsum * gate_row * (1.0 - gate_row)).astype(jnp.bfloat16).astype(jnp.float32)
        gg[pl.ds(q, 1), :] = ggrad
        delta = jnp.sum(da_t * att_t, axis=0, keepdims=True)
        dp = dot(vals, da, NT)
        ds = (probs * (dp - delta)).astype(jnp.bfloat16)
        terms_k[q, :SEL] = (dot(ds, qc, NN) * SCALE).reshape(SEL, BLK, HD)
        ds_ref[q] = ds
        return c

    def query(q):
        rows = slice(q * BLK, (q + 1) * BLK)
        dq = (dot(kc[q], ds_ref[q], TN) * SCALE).T.astype(jnp.bfloat16)
        for h in range(GQA):
            dq_ref[rows, lanes[h]] = dq[h * BLK : (h + 1) * BLK]

    def give(t, r, m):
        return copy(snd.at[t, r, m], rx.at[t, r, m], y_s.at[t, r, m], y_r.at[t, r, m], mate(m))

    def summed(t, slot):
        total = terms[t][0, pos_s[slot, lane]]
        for q in range(1, QB):
            total = total + terms[t][q, pos_s[slot, lane + q]]
        return total

    def send_row(t, r):
        @pl.when(y >= r)
        def _():
            def one(i, c):
                m = lax.rem(i, NW)
                snd[t, r, m] = summed(t, row_of(r) * NW + lax.rem(w + m, NW)).astype(jnp.bfloat16)

                @pl.when(m > 0)
                def _():
                    give(t, r, m).start()

                return c

            lax.fori_loop(1, NW + 1, one, 0)

    def far_give(t, o):
        to = (o * NW + w, z)
        return copy(far_snd.at[t, o], far_rx.at[t, NY - 1 - y], by_s.at[t, o], by_r.at[t, NY - 1 - y], to)

    def far_given(t, j):
        return copy(far_snd.at[t, 0], far_rx.at[t, j], by_s.at[t, 0], by_r.at[t, j], up_by(1))

    def far_send(t):
        for o in range(2):

            @pl.when(y >= NY - 2 + o)
            def _(o=o):
                def one(i, c):
                    far_snd[t, o, i] = summed(t, o * NW + i).astype(jnp.bfloat16)
                    return c

                lax.fori_loop(0, NW, one, 0)
                far_give(t, o).start()

    def far_deal(t, j, m):
        return copy(
            far_rx.at[t, j, lax.rem(w + m, NW)], far_in.at[t, j, m], bx_s.at[t, j, m], bx_r.at[t, j, m], mate(m)
        )

    def far_relay(t):
        for j in range(2):

            @pl.when(y < 2 - j)
            def _(j=j):
                far_given(t, j).wait_recv()

                def one(m, c):
                    far_deal(t, j, m).start()
                    return c

                lax.fori_loop(1, NW, one, 0)

    def sorted_sum(vals, row, devs):
        totals = [None] * QB
        for m in range(NW):
            val = vals(m).astype(jnp.float32)
            which = asked(row, devs(m))
            for j in range(QB):
                part = jnp.where(which == j, val, 0.0)
                totals[j] = part if m == 0 else totals[j] + part
        return totals

    def reduced(t, r):
        def wait(m, c):
            give(t, r, m).wait_recv()
            return c

        lax.fori_loop(1, NW, wait, 0)
        return sorted_sum(
            lambda m: snd[t, r, 0] if m == 0 else rx[t, r, m],
            row_of(r),
            lambda m: y * NW + lax.rem(w + NW - m, NW),
        )

    def hop(t, r, j):
        return copy(sum_out.at[t, r, j], sum_in.at[t, r, j], d_s.at[t, r, j], d_r.at[t, r, j], up_by(-1))

    def hop_in(t, r, j):
        @pl.when(y < NY - 1)
        def _():
            hop(t, r, j).wait_recv()

    def no_hop_in(t, r):
        @pl.when(y >= NY - 1)
        def _():
            sum_in[t, r] = jnp.zeros((QB, BLK, HD), jnp.bfloat16)

    def pass_on(t, r):
        @pl.when(y >= r)
        def _():
            totals = reduced(t, r)
            if r < REACH - 1:
                no_hop_in(t, r + 1)
            for j in range(QB):
                val = totals[j]
                if r < REACH - 1:
                    hop_in(t, r + 1, j)
                    val = val + sum_in[t, r + 1, j].astype(jnp.float32)
                sum_out[t, r, j] = val.astype(jnp.bfloat16)
                hop(t, r, j).start()

    def finish(t, ref):
        totals = reduced(t, 0)
        for j in range(QB):
            fin[j] = totals[j] + summed(t, NSEQ + j)
        for i in range(2):

            @pl.when(y < 2 - i)
            def _(i=i):
                def wait(m, c):
                    far_deal(t, i, m).wait_recv()
                    return c

                lax.fori_loop(1, NW, wait, 0)
                more = sorted_sum(
                    lambda m: far_rx[t, i, w] if m == 0 else far_in[t, i, m],
                    y,
                    lambda m: far_row(i) * NW + lax.rem(w + NW - m, NW),
                )
                for j in range(QB):
                    fin[j] += more[j]

        no_hop_in(t, 1)
        for j in range(QB):
            hop_in(t, 1, j)
            val = fin[j] + sum_in[t, 1, j].astype(jnp.float32)
            ref[j] = val.astype(jnp.bfloat16)

    order = (5, 4, 3, 2, 1, 0)

    all_in(0)
    lax.fori_loop(0, QB, score, 0)
    send_row(1, 5)
    far_send(1)
    for r in order[1:]:
        send_row(1, r)
    all_in(1)
    lax.fori_loop(0, QB // 2, attend, 0)
    pass_on(1, 5)
    lax.fori_loop(QB // 2, QB, attend, 0)
    send_row(0, 5)
    send_row(0, 4)
    far_send(0)
    for r in order[2:]:
        send_row(0, r)

    gbuf[z] = jnp.zeros((8, QB * BLK), jnp.float32)
    for q in range(QB):
        for h in range(GQA):
            gbuf[z, h : h + 1, q * BLK : (q + 1) * BLK] = gg[q : q + 1, h * BLK : (h + 1) * BLK]

    def gate_up(d):
        at = gbuf.at[lax.rem(z + NZ - max(d - 2, 0), NZ)]
        return copy(at, at, gu_s.at[d - 1], gu_r.at[d - 1], ahead[min(d, 2) - 1])

    def gate_up_in(d):
        at = gbuf.at[lax.rem(z + NZ - d, NZ)]
        return copy(at, at, gu_s.at[d - 1], gu_r.at[d - 1], ahead[min(d, 2) - 1])

    def gate_down(d):
        at = gbuf.at[lax.rem(z + max(d - 2, 0), NZ)]
        return copy(at, at, gd_s.at[d - 1], gd_r.at[d - 1], behind[min(d, 2) - 1])

    def gate_down_in(d):
        at = gbuf.at[lax.rem(z + d, NZ)]
        return copy(at, at, gd_s.at[d - 1], gd_r.at[d - 1], behind[min(d, 2) - 1])

    for d in (1, 2):
        gate_up(d).start()
        gate_down(d).start()

    def gate_step(k):
        for d in (2 * k - 1, 2 * k):
            gate_up_in(d).wait_recv()
            if d + 2 <= 8:
                gate_up(d + 2).start()
            if d <= 7:
                gate_down_in(d).wait_recv()
                if d + 2 <= 7:
                    gate_down(d + 2).start()

    pass_on(1, 4)
    far_relay(1)
    pass_on(0, 5)
    query(0)
    pass_on(1, 3)
    gate_step(1)
    pass_on(0, 4)
    query(1)
    pass_on(1, 2)
    gate_step(2)
    pass_on(0, 3)
    query(2)
    far_relay(0)
    pass_on(1, 1)
    pass_on(0, 2)
    query(3)
    dq_out = pltpu.make_async_copy(dq_ref, dq_hbm, out_s.at[0])
    dq_out.start()
    gate_step(3)
    finish(1, dv_ref)
    pass_on(0, 1)
    gate_step(4)
    gates = gbuf[...].reshape(NZ * 8, QB * BLK).astype(jnp.bfloat16)
    gi_ref[...] = dot(gwp[...].astype(jnp.bfloat16), gates, TN).astype(jnp.bfloat16)
    gi_out = pltpu.make_async_copy(gi_ref, gi_hbm, out_s.at[1])
    gi_out.start()
    finish(0, dk_ref)

    for t in range(2):
        for r in range(1, REACH):

            @pl.when((y >= r - 1) & (y < NY - 1))
            def _(t=t, r=r):
                for c in range(CUTS):
                    spread(t, r, c).wait_send()

            @pl.when(y >= r)
            def _(t=t, r=r):
                for j in range(QB):
                    hop(t, r, j).wait_send()

        for r in range(REACH):

            @pl.when(y >= r)
            def _(t=t, r=r):
                def sent(m, c):
                    fetch(t, r, m).wait_send()
                    give(t, r, m).wait_send()
                    return c

                lax.fori_loop(1, NW, sent, 0)

        for j in range(2):

            @pl.when(y < 2 - j)
            def _(t=t, j=j):
                def sent(m, c):
                    far_fetch(t, j, m).wait_send()
                    far_deal(t, j, m).wait_send()
                    return c

                lax.fori_loop(1, NW, sent, 0)
                far_push(t, j).wait_send()

            @pl.when(y >= NY - 2 + j)
            def _(t=t, j=j):
                far_give(t, j).wait_send()

    for d in range(1, 9):
        gate_up(d).wait_send()
        if d < 8:
            gate_down(d).wait_send()
    dq_out.wait()
    gi_out.wait()


def place(*refs):
    half = len(refs) // 2
    for src, dst in zip(refs[:half], refs[half:]):
        dst[...] = src[...]


def shards(queries, keys, values, grad_out, gate, gate_weight, selection):
    vmem = pl.BlockSpec(memory_space=pltpu.VMEM)
    hbm = pl.BlockSpec(memory_space=pl.ANY)
    bf, f32, i32 = jnp.bfloat16, jnp.float32, jnp.int32
    dma = pltpu.SemaphoreType.DMA
    blocks = (QB, BLK, HD)
    tokens, width = queries.shape
    depth = gate_weight.shape[1]
    outs = (
        jax.ShapeDtypeStruct(queries.shape, bf),
        jax.ShapeDtypeStruct(blocks, bf),
        jax.ShapeDtypeStruct(blocks, bf),
        jax.ShapeDtypeStruct((depth, tokens), bf),
    )
    results = pl.pallas_call(
        kernel,
        out_shape=outs,
        in_specs=[hbm] * 7,
        out_specs=(hbm, vmem, vmem, hbm),
        scratch_shapes=[pltpu.VMEM(blocks, bf) for _ in range(2 * REACH)]
        + [
            pltpu.VMEM((tokens, width), bf),
            pltpu.VMEM((tokens, width), bf),
            pltpu.VMEM((GQA, tokens), f32),
            pltpu.VMEM((NZ * GQA, depth), bf),
            pltpu.VMEM((SEL, NSEQ * QB), i32),
            pltpu.VMEM((tokens, width), bf),
            pltpu.VMEM((depth, tokens), bf),
            pltpu.VMEM((QB, SEL * BLK, GQA * BLK), bf),
            pltpu.VMEM((NY + SEL + NSEQ + 8, NSEQ * QB), i32),
            pltpu.SMEM((NY, NSEQ * QB), i32),
            pltpu.SMEM((SEL, HD), i32),
            pltpu.SMEM((NSEQ + 8, HD), i32),
            pltpu.VMEM((2, REACH, NW, BLK, HD), bf),
            pltpu.VMEM((NSEQ + QB, BLK, HD), bf),
            pltpu.VMEM((NSEQ + QB, BLK, HD), bf),
            pltpu.VMEM((QB, SEL * BLK, HD), bf),
            pltpu.VMEM((SEL * BLK, HD), bf),
            pltpu.VMEM((QB, SEL * BLK, GQA * BLK), f32),
            pltpu.VMEM((QB, GQA * BLK, HD), bf),
            pltpu.VMEM((QB, GQA * BLK, HD), bf),
            pltpu.VMEM((QB, SEL + 1, BLK, HD), f32),
            pltpu.VMEM((QB, SEL + 1, BLK, HD), f32),
            pltpu.VMEM((8, GQA * BLK), f32),
            pltpu.VMEM((8, GQA * BLK), f32),
            pltpu.VMEM((NZ, 8, QB * BLK), f32),
            pltpu.VMEM((NZ * 8, depth), f32),
            pltpu.VMEM((2, REACH, NW, BLK, HD), bf),
            pltpu.VMEM((2, REACH, NW, BLK, HD), bf),
            pltpu.VMEM((2, REACH) + blocks, bf),
            pltpu.VMEM((2, REACH) + blocks, bf),
            pltpu.VMEM(blocks, f32),
            pltpu.VMEM((2, 2, NW, BLK, HD), bf),
            pltpu.VMEM((2, 2, NW, BLK, HD), bf),
            pltpu.VMEM((2, 2, NW, BLK, HD), bf),
            pltpu.VMEM((2, 2, NW, BLK, HD), bf),
            pltpu.VMEM((2, 2, NW, BLK, HD), bf),
            dma((9,)), dma((2,)), dma((3,)),
            dma((2, REACH, CUTS)), dma((2, REACH, CUTS)),
            dma((2, REACH, NW)), dma((2, REACH, NW)), dma((2, REACH, NW)), dma((2, REACH, NW)),
            dma((2, REACH, QB)), dma((2, REACH, QB)),
            dma((8,)), dma((8,)), dma((7,)), dma((7,)),
            dma((2, 2, NW)), dma((2, 2, NW)), dma((2, 2)), dma((2, 2)),
            dma((2, 2)), dma((2, 2)), dma((2, 2, NW)), dma((2, 2, NW)),
        ],
        compiler_params=pltpu.CompilerParams(
            collective_id=0, has_side_effects=True, vmem_limit_bytes=56 << 20
        ),
    )(
        queries,
        keys.reshape(blocks),
        values.reshape(blocks),
        grad_out,
        gate.T,
        gate_weight,
        selection.transpose(1, 2, 0)[0],
    )
    dq, dk, dv, gi = pl.pallas_call(
        place,
        out_shape=outs,
        in_specs=[vmem] * 4,
        out_specs=(vmem,) * 4,
        compiler_params=pltpu.CompilerParams(vmem_limit_bytes=56 << 20),
    )(*results)
    return dq, dk.reshape(keys.shape), dv.reshape(values.shape), gi.T


def solution(mesh):
    placed = (
        P("seq", "head"),
        P("seq", "head"),
        P("seq", "head"),
        P("seq", "head"),
        P("seq", "head"),
        P(None, "head"),
        P(None, "head", None),
    )
    return jax.shard_map(
        shards,
        mesh=mesh,
        in_specs=placed,
        out_specs=(P("seq", "head"), P("seq", "head"), P("seq", "head"), P("seq", "head")),
        check_vma=False,
    )
```

```python
import functools
import math

import jax
import jax.numpy as jnp
from jax import lax
from jax.experimental import pallas as pl
from jax.experimental.pallas import tpu as pltpu
from jax.sharding import PartitionSpec as P

BLK = 64
HD = 128
QB = 4
SEL = 16
GQA = 4
NY = 8
NW = 8
NZ = 16
NSEQ = NY * NW
REACH = 6
CUTS = 4
MESH = pl.DeviceIdType.MESH
SCALE = 1.0 / math.sqrt(HD)
EXP2_SCALE = SCALE / math.log(2.0)


def dot(a, b, dims):
    return lax.dot_general(a, b, (dims, ((), ())), preferred_element_type=jnp.float32)


NN = ((1,), (0,))
NT = ((1,), (1,))
TN = ((0,), (0,))


def kernel(
    q_hbm, k_hbm, v_hbm, g_hbm, gate_hbm, gw_hbm, sel_hbm,
    dq_hbm, dk_ref, dv_ref, gi_hbm,
    *scratch,
):
    cols = (scratch[:REACH], scratch[REACH : 2 * REACH])
    (
        q_ref, g_ref, gate_ref, gw_ref, sel_ref, dq_ref, gi_ref,
        ds_ref, tbl, req_s, code_s, pos_s,
        stage, tab_k, tab_v, kc, vc, probs_ref, qc_ref, da_ref, terms_k, terms_v,
        gr, gg, gbuf, gwp, snd, rx, sum_out, sum_in, fin,
        far_stage, far_tab, far_snd, far_rx, far_in,
        in_s, out_s, t_s, f_s, f_r, x_s, x_r, y_s, y_r, d_s, d_r, gu_s, gu_r, gd_s, gd_r,
        fx_s, fx_r, fy_s, fy_r, by_s, by_r, bx_s, bx_r,
    ) = scratch[2 * REACH :]
    tab = (tab_k, tab_v)
    terms = (terms_k, terms_v)
    s = lax.axis_index("seq")
    z = lax.axis_index("head")
    y = s // NW
    w = lax.rem(s, NW)

    def mate(m):
        return (y * NW + lax.rem(w + m, NW), z)

    def row_of(r):
        return lax.rem(y + (NY - r), NY)

    def up_by(n):
        return (lax.rem(y + n + NY, NY) * NW + w, z)

    ahead = [(s, lax.rem(z + i, NZ)) for i in (1, 2)]
    behind = [(s, lax.rem(z + NZ - i, NZ)) for i in (1, 2)]

    barrier = pltpu.get_barrier_semaphore()
    for m in range(1, NW):
        pl.semaphore_signal(barrier, inc=1, device_id=mate(m), device_id_type=MESH)
    for to in (up_by(1), up_by(-1), up_by(2), up_by(-2), *ahead, *behind):
        pl.semaphore_signal(barrier, inc=1, device_id=to, device_id_type=MESH)

    loads = [
        pltpu.make_async_copy(a, b, in_s.at[i])
        for i, (a, b) in enumerate(
            (
                (k_hbm, cols[0][0]), (v_hbm, cols[1][0]), (sel_hbm, sel_ref),
                (k_hbm, tab_k.at[pl.ds(NSEQ, QB)]), (v_hbm, tab_v.at[pl.ds(NSEQ, QB)]),
                (gate_hbm, gate_ref), (g_hbm, g_ref), (q_hbm, q_ref), (gw_hbm, gw_ref),
            )
        )
    ]
    for load in loads:
        load.start()

    loads[2].wait()
    sel = sel_ref[...]
    owner = jnp.right_shift(sel, 2)
    inner = jnp.bitwise_and(sel, 3)
    code = jnp.where(owner == s, NSEQ + inner, owner)
    mine = lax.broadcasted_iota(jnp.int32, (NY, NSEQ * QB), 0) * NW + w
    slots = lax.broadcasted_iota(jnp.int32, (NSEQ + 8, NSEQ * QB), 0)
    req = jnp.full((NY, NSEQ * QB), -1, jnp.int32)
    for p in range(SEL):
        req = jnp.where(owner[p : p + 1] == mine, inner[p : p + 1], req)
    tbl[0:NY] = req
    half = pl.ds(pl.multiple_of(y // 4 * HD, HD), HD)
    req_in = pltpu.make_async_copy(tbl.at[pl.ds(0, NY)], req_s, t_s.at[0])
    req_in.start()
    pos = jnp.full((NSEQ + 8, NSEQ * QB), SEL, jnp.int32)
    for p in range(SEL):
        pos = jnp.where(code[p : p + 1] == slots, p, pos)
    tbl[NY : NY + SEL] = code
    tbl[NY + SEL :] = pos
    code_in = pltpu.make_async_copy(tbl.at[pl.ds(NY, SEL), half], code_s, t_s.at[1])
    pos_in = pltpu.make_async_copy(tbl.at[pl.ds(NY + SEL, NSEQ + 8), half], pos_s, t_s.at[2])
    code_in.start()
    pos_in.start()
    lane = lax.rem(s * QB, HD)

    def asked(row, d):
        got = req_s[row, d * QB]
        for q in range(1, QB):
            got = jnp.maximum(got, req_s[row, d * QB + q])
        return got

    loads[0].wait()
    loads[1].wait()
    pl.semaphore_wait(barrier, NW + 7)

    def copy(src, dst, send, recv, to):
        return pltpu.make_async_remote_copy(
            src_ref=src, dst_ref=dst, send_sem=send, recv_sem=recv, device_id=to, device_id_type=MESH
        )

    def spread(t, r, c):
        part = pl.ds(c * (QB // CUTS), QB // CUTS)
        return copy(
            cols[t][r - 1].at[part], cols[t][r].at[part], f_s.at[t, r, c], f_r.at[t, r, c], up_by(1)
        )

    def spread_start(t, r, c):
        @pl.when((y >= r - 1) & (y < NY - 1))
        def _():
            spread(t, r, c).start()

    def spread_in(t, r, c):
        @pl.when(y >= r)
        def _():
            spread(t, r, c).wait_recv()

    def fetch(t, r, m):
        return copy(stage.at[t, r, m], tab[t].at[row_of(r) * NW + w], x_s.at[t, r, m], x_r.at[t, r, m], mate(m))

    def arrive(t, r, m):
        home = row_of(r) * NW + lax.rem(w + NW - m, NW)
        return copy(stage.at[t, r, m], tab[t].at[home], x_s.at[t, r, m], x_r.at[t, r, m], mate(m))

    def hand_out(t, r):
        @pl.when(y >= r)
        def _():
            row = row_of(r)
            tab[t][row * NW + w] = cols[t][r][jnp.maximum(asked(row, s), 0)]

            def one(m, c):
                block = jnp.maximum(asked(row, y * NW + lax.rem(w + m, NW)), 0)
                stage[t, r, m] = cols[t][r][block]
                fetch(t, r, m).start()
                return c

            lax.fori_loop(1, NW, one, 0)

    def far_row(j):
        return NY - 1 - j

    def far_fetch(t, j, m):
        return copy(far_stage.at[t, j, m], far_tab.at[t, j, w], fx_s.at[t, j, m], fx_r.at[t, j, m], mate(m))

    def far_arrive(t, j, m):
        at = lax.rem(w + NW - m, NW)
        return copy(far_stage.at[t, j, m], far_tab.at[t, j, at], fx_s.at[t, j, m], fx_r.at[t, j, m], mate(m))

    def far_push(t, j):
        return copy(
            far_tab.at[t, j], tab[t].at[pl.ds(y * NW, NW)], fy_s.at[t, j], fy_r.at[t, y], (far_row(j) * NW + w, z)
        )

    def far_landed(t, o):
        return copy(far_tab.at[t, 0], tab[t].at[pl.ds(o * NW, NW)], fy_s.at[t, 0], fy_r.at[t, o], up_by(1))

    def far_hand_out(t):
        for j in range(2):

            @pl.when(y < 2 - j)
            def _(j=j):
                far_tab[t, j, w] = cols[t][0][jnp.maximum(asked(y, far_row(j) * NW + w), 0)]

                def one(m, c):
                    block = jnp.maximum(asked(y, far_row(j) * NW + lax.rem(w + m, NW)), 0)
                    far_stage[t, j, m] = cols[t][0][block]
                    far_fetch(t, j, m).start()
                    return c

                lax.fori_loop(1, NW, one, 0)

    def far_forward(t):
        for j in range(2):

            @pl.when(y < 2 - j)
            def _(j=j):
                def landed(m, c):
                    far_arrive(t, j, m).wait_recv()
                    return c

                lax.fori_loop(1, NW, landed, 0)
                far_push(t, j).start()

    for c in range(CUTS):
        for t in range(2):
            spread_start(t, 1, c)
    req_in.wait()
    for t in range(2):
        far_hand_out(t)
        hand_out(t, 0)
    for k in range(1, REACH + 1):
        if k < REACH:
            for c in range(CUTS):
                spread_in(0, k, c)
                if k < REACH - 1:
                    spread_start(0, k + 1, c)
            hand_out(0, k)
        if k > 1:
            for c in range(CUTS):
                spread_in(1, k - 1, c)
                if k < REACH:
                    spread_start(1, k, c)
            hand_out(1, k - 1)
        if k < 3:
            far_forward(k - 1)

    none = jnp.zeros((BLK, HD), jnp.float32)
    for q in range(QB):
        terms_k[q, SEL] = none
        terms_v[q, SEL] = none
    for load in loads[3:]:
        load.wait()
    for q in range(QB):
        for h in range(GQA):
            gr[q : q + 1, h * BLK : (h + 1) * BLK] = gate_ref[h : h + 1, q * BLK : (q + 1) * BLK]
    gwp[...] = jnp.zeros_like(gwp)
    gw = gw_ref[...].astype(jnp.float32)
    for i in range(NZ):
        gwp[8 * i : 8 * i + GQA] = gw[GQA * i : GQA * (i + 1)]
    code_in.wait()
    pos_in.wait()

    def all_in(t):
        for r in range(REACH):

            @pl.when(y >= r)
            def _(r=r):
                def landed(m, c):
                    arrive(t, r, m).wait_recv()
                    return c

                lax.fori_loop(1, NW, landed, 0)

        for o in range(2):

            @pl.when(y >= NY - 2 + o)
            def _(o=o):
                far_landed(t, o).wait_recv()

    lanes = [slice(h * HD, (h + 1) * HD) for h in range(GQA)]
    below_diag = lax.broadcasted_iota(jnp.int32, (BLK, GQA * BLK), 0) - lax.rem(
        lax.broadcasted_iota(jnp.int32, (BLK, GQA * BLK), 1), BLK
    )

    def gather(t, q, p):
        at = code_s[p, lane + q]
        return tab[t][jnp.where(at < 0, NSEQ, at)]

    def gate_of(q):
        row = gr[pl.ds(q, 1), :]
        return row, jnp.broadcast_to(row, (HD, GQA * BLK))

    def score(q, c):
        rows = pl.ds(pl.multiple_of(q * BLK, BLK), BLK)
        qc = jnp.concatenate([q_ref[rows, a] for a in lanes], axis=0)
        gf = jnp.concatenate([g_ref[rows, a] for a in lanes], axis=0).astype(jnp.float32)
        da = (gate_of(q)[1].T * gf).astype(jnp.bfloat16)
        qc_ref[q] = qc
        da_ref[q] = da
        for p in range(SEL):
            kc[q, p * BLK : (p + 1) * BLK] = gather(0, q, p)
        st = dot(kc[q], qc, NT)
        parts = []
        for p in range(SEL):
            at = code_s[p, lane + q]
            reach = jnp.where(at == NSEQ + q, 0, jnp.where(at < 0, -BLK, BLK))
            parts.append(jnp.where(below_diag <= reach, st[p * BLK : (p + 1) * BLK], -jnp.inf))
        st = jnp.concatenate(parts, axis=0)
        top = jnp.max(st, axis=0, keepdims=True)
        e = jnp.exp2((st - top) * EXP2_SCALE)
        probs = e * (1.0 / jnp.sum(e, axis=0, keepdims=True))
        probs_ref[q] = probs
        terms_v[q, :SEL] = dot(probs.astype(jnp.bfloat16), da, NN).reshape(SEL, BLK, HD)
        return c

    def attend(q, c):
        rows = pl.ds(pl.multiple_of(q * BLK, BLK), BLK)
        for p in range(SEL):
            vc[p * BLK : (p + 1) * BLK] = gather(1, q, p)
        vals = vc[...]
        probs = probs_ref[q]
        qc = qc_ref[q]
        da = da_ref[q]
        att_t = dot(vals, probs.astype(jnp.bfloat16), TN)
        g_t = jnp.concatenate([g_ref[rows, a] for a in lanes], axis=0).astype(jnp.float32).T
        gate_row, gate_t = gate_of(q)
        da_t = (gate_t * g_t).astype(jnp.bfloat16).astype(jnp.float32)
        gsum = jnp.sum(g_t * att_t, axis=0, keepdims=True)
        ggrad = (gsum * gate_row * (1.0 - gate_row)).astype(jnp.bfloat16).astype(jnp.float32)
        gg[pl.ds(q, 1), :] = ggrad
        delta = jnp.sum(da_t * att_t, axis=0, keepdims=True)
        dp = dot(vals, da, NT)
        ds = (probs * (dp - delta)).astype(jnp.bfloat16)
        terms_k[q, :SEL] = (dot(ds, qc, NN) * SCALE).reshape(SEL, BLK, HD)
        ds_ref[q] = ds
        return c

    def query(q):
        rows = slice(q * BLK, (q + 1) * BLK)
        dq = (dot(kc[q], ds_ref[q], TN) * SCALE).T.astype(jnp.bfloat16)
        for h in range(GQA):
            dq_ref[rows, lanes[h]] = dq[h * BLK : (h + 1) * BLK]

    def give(t, r, m):
        return copy(snd.at[t, r, m], rx.at[t, r, m], y_s.at[t, r, m], y_r.at[t, r, m], mate(m))

    def summed(t, slot):
        total = terms[t][0, pos_s[slot, lane]]
        for q in range(1, QB):
            total = total + terms[t][q, pos_s[slot, lane + q]]
        return total

    def send_row(t, r):
        @pl.when(y >= r)
        def _():
            def one(i, c):
                m = lax.rem(i, NW)
                snd[t, r, m] = summed(t, row_of(r) * NW + lax.rem(w + m, NW)).astype(jnp.bfloat16)

                @pl.when(m > 0)
                def _():
                    give(t, r, m).start()

                return c

            lax.fori_loop(1, NW + 1, one, 0)

    def far_give(t, o):
        to = (o * NW + w, z)
        return copy(far_snd.at[t, o], far_rx.at[t, NY - 1 - y], by_s.at[t, o], by_r.at[t, NY - 1 - y], to)

    def far_given(t, j):
        return copy(far_snd.at[t, 0], far_rx.at[t, j], by_s.at[t, 0], by_r.at[t, j], up_by(1))

    def far_send(t):
        for o in range(2):

            @pl.when(y >= NY - 2 + o)
            def _(o=o):
                def one(i, c):
                    far_snd[t, o, i] = summed(t, o * NW + i).astype(jnp.bfloat16)
                    return c

                lax.fori_loop(0, NW, one, 0)
                far_give(t, o).start()

    def far_deal(t, j, m):
        return copy(
            far_rx.at[t, j, lax.rem(w + m, NW)], far_in.at[t, j, m], bx_s.at[t, j, m], bx_r.at[t, j, m], mate(m)
        )

    def far_relay(t):
        for j in range(2):

            @pl.when(y < 2 - j)
            def _(j=j):
                far_given(t, j).wait_recv()

                def one(m, c):
                    far_deal(t, j, m).start()
                    return c

                lax.fori_loop(1, NW, one, 0)

    def sorted_sum(vals, row, devs):
        totals = [None] * QB
        for m in range(NW):
            val = vals(m).astype(jnp.float32)
            which = asked(row, devs(m))
            for j in range(QB):
                part = jnp.where(which == j, val, 0.0)
                totals[j] = part if m == 0 else totals[j] + part
        return totals

    def reduced(t, r):
        def wait(m, c):
            give(t, r, m).wait_recv()
            return c

        lax.fori_loop(1, NW, wait, 0)
        return sorted_sum(
            lambda m: snd[t, r, 0] if m == 0 else rx[t, r, m],
            row_of(r),
            lambda m: y * NW + lax.rem(w + NW - m, NW),
        )

    def hop(t, r, j):
        return copy(sum_out.at[t, r, j], sum_in.at[t, r, j], d_s.at[t, r, j], d_r.at[t, r, j], up_by(-1))

    def hop_in(t, r, j):
        @pl.when(y < NY - 1)
        def _():
            hop(t, r, j).wait_recv()

    def no_hop_in(t, r):
        @pl.when(y >= NY - 1)
        def _():
            sum_in[t, r] = jnp.zeros((QB, BLK, HD), jnp.bfloat16)

    def pass_on(t, r):
        @pl.when(y >= r)
        def _():
            totals = reduced(t, r)
            if r < REACH - 1:
                no_hop_in(t, r + 1)
            for j in range(QB):
                val = totals[j]
                if r < REACH - 1:
                    hop_in(t, r + 1, j)
                    val = val + sum_in[t, r + 1, j].astype(jnp.float32)
                sum_out[t, r, j] = val.astype(jnp.bfloat16)
                hop(t, r, j).start()

    def finish(t, ref):
        totals = reduced(t, 0)
        for j in range(QB):
            fin[j] = totals[j] + summed(t, NSEQ + j)
        for i in range(2):

            @pl.when(y < 2 - i)
            def _(i=i):
                def wait(m, c):
                    far_deal(t, i, m).wait_recv()
                    return c

                lax.fori_loop(1, NW, wait, 0)
                more = sorted_sum(
                    lambda m: far_rx[t, i, w] if m == 0 else far_in[t, i, m],
                    y,
                    lambda m: far_row(i) * NW + lax.rem(w + NW - m, NW),
                )
                for j in range(QB):
                    fin[j] += more[j]

        no_hop_in(t, 1)
        for j in range(QB):
            hop_in(t, 1, j)
            val = fin[j] + sum_in[t, 1, j].astype(jnp.float32)
            ref[j] = val.astype(jnp.bfloat16)

    order = (5, 4, 3, 2, 1, 0)

    all_in(0)
    lax.fori_loop(0, QB, score, 0)
    send_row(1, 5)
    far_send(1)
    for r in order[1:]:
        send_row(1, r)
    all_in(1)
    lax.fori_loop(0, QB // 2, attend, 0)
    pass_on(1, 5)
    lax.fori_loop(QB // 2, QB, attend, 0)
    send_row(0, 5)
    send_row(0, 4)
    far_send(0)
    for r in order[2:]:
        send_row(0, r)

    gbuf[z] = jnp.zeros((8, QB * BLK), jnp.float32)
    for q in range(QB):
        for h in range(GQA):
            gbuf[z, h : h + 1, q * BLK : (q + 1) * BLK] = gg[q : q + 1, h * BLK : (h + 1) * BLK]

    def gate_up(d):
        at = gbuf.at[lax.rem(z + NZ - max(d - 2, 0), NZ)]
        return copy(at, at, gu_s.at[d - 1], gu_r.at[d - 1], ahead[min(d, 2) - 1])

    def gate_up_in(d):
        at = gbuf.at[lax.rem(z + NZ - d, NZ)]
        return copy(at, at, gu_s.at[d - 1], gu_r.at[d - 1], ahead[min(d, 2) - 1])

    def gate_down(d):
        at = gbuf.at[lax.rem(z + max(d - 2, 0), NZ)]
        return copy(at, at, gd_s.at[d - 1], gd_r.at[d - 1], behind[min(d, 2) - 1])

    def gate_down_in(d):
        at = gbuf.at[lax.rem(z + d, NZ)]
        return copy(at, at, gd_s.at[d - 1], gd_r.at[d - 1], behind[min(d, 2) - 1])

    for d in (1, 2):
        gate_up(d).start()
        gate_down(d).start()

    def gate_step(k):
        for d in (2 * k - 1, 2 * k):
            gate_up_in(d).wait_recv()
            if d + 2 <= 8:
                gate_up(d + 2).start()
            if d <= 7:
                gate_down_in(d).wait_recv()
                if d + 2 <= 7:
                    gate_down(d + 2).start()

    def fetch_sent(t):
        for r in range(1, REACH):

            @pl.when((y >= r - 1) & (y < NY - 1))
            def _(r=r):
                for c in range(CUTS):
                    spread(t, r, c).wait_send()

        for r in range(REACH):

            @pl.when(y >= r)
            def _(r=r):
                def sent(m, c):
                    fetch(t, r, m).wait_send()
                    return c

                lax.fori_loop(1, NW, sent, 0)

        for j in range(2):

            @pl.when(y < 2 - j)
            def _(j=j):
                def sent(m, c):
                    far_fetch(t, j, m).wait_send()
                    return c

                lax.fori_loop(1, NW, sent, 0)
                far_push(t, j).wait_send()

    def sums_sent(t):
        for r in range(REACH):

            @pl.when(y >= r)
            def _(r=r):
                def sent(m, c):
                    give(t, r, m).wait_send()
                    return c

                lax.fori_loop(1, NW, sent, 0)
                if r > 0:
                    for j in range(QB):
                        hop(t, r, j).wait_send()

        for j in range(2):

            @pl.when(y < 2 - j)
            def _(j=j):
                def sent(m, c):
                    far_deal(t, j, m).wait_send()
                    return c

                lax.fori_loop(1, NW, sent, 0)

            @pl.when(y >= NY - 2 + j)
            def _(j=j):
                far_give(t, j).wait_send()

    pass_on(1, 4)
    far_relay(1)
    pass_on(0, 5)
    query(0)
    pass_on(1, 3)
    gate_step(1)
    pass_on(0, 4)
    query(1)
    fetch_sent(0)
    pass_on(1, 2)
    gate_step(2)
    pass_on(0, 3)
    query(2)
    fetch_sent(1)
    far_relay(0)
    pass_on(1, 1)
    pass_on(0, 2)
    query(3)
    dq_out = pltpu.make_async_copy(dq_ref, dq_hbm, out_s.at[0])
    dq_out.start()
    gate_step(3)
    finish(1, dv_ref)
    pass_on(0, 1)
    gate_step(4)
    gates = gbuf[...].reshape(NZ * 8, QB * BLK).astype(jnp.bfloat16)
    gi_ref[...] = dot(gwp[...].astype(jnp.bfloat16), gates, TN).astype(jnp.bfloat16)
    gi_out = pltpu.make_async_copy(gi_ref, gi_hbm, out_s.at[1])
    gi_out.start()
    sums_sent(1)
    for d in range(1, 9):
        gate_up(d).wait_send()
        if d < 8:
            gate_down(d).wait_send()
    sums_sent(0)
    finish(0, dk_ref)

    dq_out.wait()
    gi_out.wait()


def place(*refs):
    half = len(refs) // 2
    for src, dst in zip(refs[:half], refs[half:]):
        dst[...] = src[...]


def shards(queries, keys, values, grad_out, gate, gate_weight, selection):
    vmem = pl.BlockSpec(memory_space=pltpu.VMEM)
    hbm = pl.BlockSpec(memory_space=pl.ANY)
    bf, f32, i32 = jnp.bfloat16, jnp.float32, jnp.int32
    dma = pltpu.SemaphoreType.DMA
    blocks = (QB, BLK, HD)
    tokens, width = queries.shape
    depth = gate_weight.shape[1]
    outs = (
        jax.ShapeDtypeStruct(queries.shape, bf),
        jax.ShapeDtypeStruct(blocks, bf),
        jax.ShapeDtypeStruct(blocks, bf),
        jax.ShapeDtypeStruct((depth, tokens), bf),
    )
    results = pl.pallas_call(
        kernel,
        out_shape=outs,
        in_specs=[hbm] * 7,
        out_specs=(hbm, vmem, vmem, hbm),
        scratch_shapes=[pltpu.VMEM(blocks, bf) for _ in range(2 * REACH)]
        + [
            pltpu.VMEM((tokens, width), bf),
            pltpu.VMEM((tokens, width), bf),
            pltpu.VMEM((GQA, tokens), f32),
            pltpu.VMEM((NZ * GQA, depth), bf),
            pltpu.VMEM((SEL, NSEQ * QB), i32),
            pltpu.VMEM((tokens, width), bf),
            pltpu.VMEM((depth, tokens), bf),
            pltpu.VMEM((QB, SEL * BLK, GQA * BLK), bf),
            pltpu.VMEM((NY + SEL + NSEQ + 8, NSEQ * QB), i32),
            pltpu.SMEM((NY, NSEQ * QB), i32),
            pltpu.SMEM((SEL, HD), i32),
            pltpu.SMEM((NSEQ + 8, HD), i32),
            pltpu.VMEM((2, REACH, NW, BLK, HD), bf),
            pltpu.VMEM((NSEQ + QB, BLK, HD), bf),
            pltpu.VMEM((NSEQ + QB, BLK, HD), bf),
            pltpu.VMEM((QB, SEL * BLK, HD), bf),
            pltpu.VMEM((SEL * BLK, HD), bf),
            pltpu.VMEM((QB, SEL * BLK, GQA * BLK), f32),
            pltpu.VMEM((QB, GQA * BLK, HD), bf),
            pltpu.VMEM((QB, GQA * BLK, HD), bf),
            pltpu.VMEM((QB, SEL + 1, BLK, HD), f32),
            pltpu.VMEM((QB, SEL + 1, BLK, HD), f32),
            pltpu.VMEM((8, GQA * BLK), f32),
            pltpu.VMEM((8, GQA * BLK), f32),
            pltpu.VMEM((NZ, 8, QB * BLK), f32),
            pltpu.VMEM((NZ * 8, depth), f32),
            pltpu.VMEM((2, REACH, NW, BLK, HD), bf),
            pltpu.VMEM((2, REACH, NW, BLK, HD), bf),
            pltpu.VMEM((2, REACH) + blocks, bf),
            pltpu.VMEM((2, REACH) + blocks, bf),
            pltpu.VMEM(blocks, f32),
            pltpu.VMEM((2, 2, NW, BLK, HD), bf),
            pltpu.VMEM((2, 2, NW, BLK, HD), bf),
            pltpu.VMEM((2, 2, NW, BLK, HD), bf),
            pltpu.VMEM((2, 2, NW, BLK, HD), bf),
            pltpu.VMEM((2, 2, NW, BLK, HD), bf),
            dma((9,)), dma((2,)), dma((3,)),
            dma((2, REACH, CUTS)), dma((2, REACH, CUTS)),
            dma((2, REACH, NW)), dma((2, REACH, NW)), dma((2, REACH, NW)), dma((2, REACH, NW)),
            dma((2, REACH, QB)), dma((2, REACH, QB)),
            dma((8,)), dma((8,)), dma((7,)), dma((7,)),
            dma((2, 2, NW)), dma((2, 2, NW)), dma((2, 2)), dma((2, 2)),
            dma((2, 2)), dma((2, 2)), dma((2, 2, NW)), dma((2, 2, NW)),
        ],
        compiler_params=pltpu.CompilerParams(
            collective_id=0, has_side_effects=True, vmem_limit_bytes=56 << 20
        ),
    )(
        queries,
        keys.reshape(blocks),
        values.reshape(blocks),
        grad_out,
        gate.T,
        gate_weight,
        selection.transpose(1, 2, 0)[0],
    )
    dq, dk, dv, gi = pl.pallas_call(
        place,
        out_shape=outs,
        in_specs=[vmem] * 4,
        out_specs=(vmem,) * 4,
        compiler_params=pltpu.CompilerParams(vmem_limit_bytes=56 << 20),
    )(*results)
    return dq, dk.reshape(keys.shape), dv.reshape(values.shape), gi.T


def solution(mesh):
    placed = (
        P("seq", "head"),
        P("seq", "head"),
        P("seq", "head"),
        P("seq", "head"),
        P("seq", "head"),
        P(None, "head"),
        P(None, "head", None),
    )
    return jax.shard_map(
        shards,
        mesh=mesh,
        in_specs=placed,
        out_specs=(P("seq", "head"), P("seq", "head"), P("seq", "head"), P("seq", "head")),
        check_vma=False,
    )
```
